128 devices in a mesh: dp: 8 (over x, core), ctx: 16 (over z, y).
Axes of the slice: x: 4, y: 4, z: 4, core: 2. Of those that a mesh axis runs over, the one named last changes fastest.
Arguments:
- queries: bfloat16 [8, 2048, 4096], P('dp', 'ctx'), may hold values from -6 to 6
- key_inputs: bfloat16 [8, 2048, 4096], P('dp', 'ctx'), may hold values from -6 to 6
- value_inputs: bfloat16 [8, 2048, 4096], P('dp', 'ctx'), may hold values from -6 to 6
- cotangent: bfloat16 [8, 2048, 4096], P('dp', 'ctx'), may hold values from -3 to 3
- filter_taps: float32 [1024, 4096], P(None, 'ctx')
- skip_gain: float32 [4096], P('ctx'), may hold values from -4 to 4
- lengths: int32 [8, 3], P('dp'), may hold values from 1 to 1024, 2048 in all within a row
Outputs:
- mixed_out: bfloat16 [8, 2048, 4096], P('dp', 'ctx')
- query_grad: bfloat16 [8, 2048, 4096], P('dp', 'ctx')
- key_grad: bfloat16 [8, 2048, 4096], P('dp', 'ctx')
- value_grad: bfloat16 [8, 2048, 4096], P('dp', 'ctx')
- filter_grad: float32 [1024, 4096], P('dp', 'ctx')
The draws below stay inside these ranges and needn't reach their ends.
Inputs may be any that keep to these rules, and one draw needn't show every extreme that they name: Each row holds the lengths of 3 windows that fill the slice of 2048 positions in order; they sum to 2048 and the largest is exactly half of 2048.
All inputs are finite; a program needn't handle non-finite values.
Results may differ from the reference program's by a relative error of at most 0.017.
Values may be sent and summed in bfloat16 or wider, within the bound.
No kernel may reach another device: no remote copies, remote signals or barrier semaphores. Data moves between devices by JAX's collectives and lax.ppermute only.
A program may use at most 192 MiB of HBM per device.

```python
import math
import jax
import jax.numpy as jnp
import numpy as np
from jax import lax

D = 4096
WINDOWS = 3
SLICES = 8
L = 2048


def draw_filter_taps(key, part):
    key = jax.random.fold_in(key, 7)
    rate_key, noise_key = jax.random.split(key)
    rates = jnp.exp(jax.random.uniform(rate_key, (D,), jnp.float32, math.log(0.5), math.log(16.0)))
    noise = jax.random.normal(noise_key, (L // 2, D), jnp.float32)
    lags = jnp.arange(L // 2, dtype=jnp.float32)[:, None]
    return jnp.sqrt(2.0 * rates[None, :] / L) * noise * jnp.exp(-rates[None, :] * lags / L)


def block_scale(rng, shape, cuts, smallest, high):
    gain = 1.0
    for dim, parts in cuts:
        heights = jax.random.uniform(jax.random.fold_in(jax.random.fold_in(rng, 6), dim), (parts,), jnp.float32, smallest / len(cuts), high / len(cuts))
        gain = gain * jnp.repeat(jnp.exp(heights), shape[dim] // parts).reshape((-1,) + (1,) * (len(shape) - 1 - dim))
    return gain


def split_up(number_of, total, bound, slope):
    portions = [(1 << 20) // math.isqrt(grade ** slope) + 1 for grade in range(2, number_of + 1)]
    rest, holding = total - bound - (number_of - 1), [1] * (number_of - 1)
    while rest > 0:
        movable = [i for i in range(number_of - 1) if holding[i] < bound]
        pool, remaining = sum([portions[i] for i in movable]), rest
        for i in movable:
            addition = min(bound - holding[i], max(1, remaining * portions[i] // pool), rest)
            holding[i] = holding[i] + addition
            rest = rest - addition
    return np.array([bound] + holding)


def uneven_parts(stream_key, amount, total, limit, lean):
    if amount == 2:
        one = jax.random.randint(stream_key, (), max(1, total - limit), min(limit, total - 1) + 1)
        return jnp.stack([one, total - one])
    tallies = jnp.asarray(split_up(amount, total, limit, lean), jnp.int32)
    pairs = (amount - 1) // 2
    giver, taker = tallies[1:1 + 2 * pairs:2], tallies[2:2 + 2 * pairs:2]
    room = jnp.minimum(giver - 1, limit - taker)
    moved = jax.random.randint(jax.random.fold_in(stream_key, 1), (pairs,), 0, 1 << 20) % (room + 1)
    tallies = tallies.at[1:1 + 2 * pairs:2].set(giver - moved).at[2:2 + 2 * pairs:2].set(taker + moved)
    return tallies[jax.random.permutation(jax.random.fold_in(stream_key, 2), amount)]


def gaussian(own_key, dims, width, limit, cuts=(), kind=jnp.bfloat16):
    factor_of = block_scale(own_key, dims, cuts, -0.22, 0.18) if cuts else 1.0
    result = jax.random.normal(own_key, dims, jnp.float32) * width * factor_of
    return jnp.minimum(jnp.maximum(result, -limit), limit).astype(kind)


def setup_inputs(seed: int = 0) -> dict:
    key_list = jax.random.split(jax.random.key(seed), 8)
    queries = gaussian(key_list[0], (SLICES, L, D), 1.0, 6.0, ((0, 8), (1, 16)))
    key_inputs = gaussian(key_list[1], (SLICES, L, D), 1.0, 6.0, ((0, 8), (1, 16)))
    value_inputs = gaussian(key_list[2], (SLICES, L, D), 1.0, 6.0, ((0, 8), (1, 16)))
    cotangent = gaussian(key_list[3], (SLICES, L, D), 0.5, 3.0, ((0, 8), (1, 16)))
    filter_taps = draw_filter_taps(jax.random.fold_in(key_list[7], 71), 0)
    skip_gain = gaussian(key_list[5], (D,), 1.0, 4.0, ((0, 16),), jnp.float32)
    lengths = jax.vmap(lambda own: uneven_parts(own, WINDOWS, L, L // 2, 0))(jax.random.split(key_list[6], SLICES)).reshape((SLICES, WINDOWS)).astype(jnp.int32)
    return {"queries": queries, "key_inputs": key_inputs, "value_inputs": value_inputs, "cotangent": cotangent, "filter_taps": filter_taps, "skip_gain": skip_gain, "lengths": lengths}


def window_masks(length_row):
    starts = jnp.cumsum(length_row) - length_row
    places = jnp.arange(L, dtype=jnp.int32)
    inside = (places[None, :] >= starts[:, None]) & (places[None, :] < (starts + length_row)[:, None])
    return inside.astype(jnp.float32)[:, :, None]


def spectrum(field):
    return jnp.fft.rfft(field, n=2 * L, axis=0)


def back_to_time(spectral):
    return jnp.fft.irfft(spectral, n=2 * L, axis=0)[:L]


def reference(queries, key_inputs, value_inputs, cotangent, filter_taps, skip_gain, lengths):
    taps_spec = spectrum(filter_taps)

    def one_slice(total, pieces):
        query_row, key_row, value_row, cot_row, length_row = pieces
        key_wide = key_row.astype(jnp.float32)
        value_wide = value_row.astype(jnp.float32)
        query_wide = query_row.astype(jnp.float32)
        cot_wide = cot_row.astype(jnp.float32)
        product = lax.optimization_barrier((key_wide * value_wide).astype(jnp.bfloat16)).astype(jnp.float32)
        masks = window_masks(length_row)
        convolved = jnp.zeros((L, D), jnp.float32)
        saved = []
        for index in range(WINDOWS):
            part = spectrum(masks[index] * product)
            saved.append(part)
            convolved = convolved + masks[index] * back_to_time(taps_spec * part)
        mixing = lax.optimization_barrier((convolved + skip_gain * product).astype(jnp.bfloat16)).astype(jnp.float32)
        mixed = (query_wide * mixing).astype(jnp.bfloat16)
        query_grad = (cot_wide * mixing).astype(jnp.bfloat16)
        delta = lax.optimization_barrier((cot_wide * query_wide).astype(jnp.bfloat16)).astype(jnp.float32)
        back = jnp.zeros((L, D), jnp.float32)
        cross = None
        for index in range(WINDOWS):
            grad_spec = spectrum(masks[index] * delta)
            back = back + masks[index] * back_to_time(jnp.conj(taps_spec) * grad_spec)
            term = grad_spec * jnp.conj(saved[index])
            cross = term if cross is None else cross + term
        units = lax.optimization_barrier((back + skip_gain * delta).astype(jnp.bfloat16)).astype(jnp.float32)
        key_grad = (units * value_wide).astype(jnp.bfloat16)
        value_grad = (units * key_wide).astype(jnp.bfloat16)
        return total + back_to_time(cross)[:L // 2], (mixed, query_grad, key_grad, value_grad)

    start = jnp.zeros((L // 2, D), jnp.float32)
    summed, outputs = lax.scan(one_slice, start, (queries, key_inputs, value_inputs, cotangent, lengths))
    mixed_out, query_grad, key_grad, value_grad = outputs
    return mixed_out, query_grad, key_grad, value_grad, summed / SLICES
```

```python
import math

import jax
import jax.numpy as jnp
import numpy as np
from jax import lax
from jax.experimental import pallas as pl
from jax.experimental.pallas import tpu as pltpu
from jax.sharding import PartitionSpec as P

BLOCK = 256
VMEM = 56 * 1024 * 1024


def transform_tables(span, half):
    places = np.arange(span)
    doubled = (2 * np.arange(half)[:, None] + 1) * places[None, :] % (2 * span)
    angle = doubled * (math.pi / span)
    rows = np.concatenate([np.cos(angle), -np.sin(angle)], 0)
    into = rows.reshape(2 * half, span // BLOCK, BLOCK).transpose(1, 0, 2)
    back = (rows.T / half).reshape(span // BLOCK, BLOCK, 2 * half)
    return into.astype(jnp.bfloat16), back.astype(jnp.bfloat16)


def cost(flops, nbytes):
    return pl.CostEstimate(flops=flops, bytes_accessed=nbytes, transcendentals=0)


def params():
    return pltpu.CompilerParams(vmem_limit_bytes=VMEM)


def pair_kernel(left_ref, right_ref, out_ref):
    width = out_ref.shape[2]
    for part in range(out_ref.shape[0]):
        cols = slice(part * width, (part + 1) * width)
        left = left_ref[:, cols].astype(jnp.float32)
        right = right_ref[:, cols].astype(jnp.float32)
        out_ref[part] = (left * right).astype(jnp.bfloat16)


def pair_product(left, right, groups):
    rows, columns = left.shape
    width = columns // groups
    steps = 4
    per = groups // steps
    return pl.pallas_call(
        pair_kernel,
        grid=(steps,),
        in_specs=[pl.BlockSpec((rows, per * width), lambda i: (0, i))] * 2,
        out_specs=pl.BlockSpec((per, rows, width), lambda i: (i, 0, 0)),
        out_shape=jax.ShapeDtypeStruct((groups, rows, width), jnp.bfloat16),
        compiler_params=params(),
        cost_estimate=cost(rows * columns, 6 * rows * columns),
        name="pair_product",
    )(left, right)


def gate_kernel(inner_ref, first_ref, second_ref, one_ref, two_ref):
    width = inner_ref.shape[2]
    for part in range(inner_ref.shape[0]):
        cols = slice(part * width, (part + 1) * width)
        inner = inner_ref[part].astype(jnp.float32)
        one_ref[:, cols] = (inner * first_ref[:, cols].astype(jnp.float32)).astype(jnp.bfloat16)
        two_ref[:, cols] = (inner * second_ref[:, cols].astype(jnp.float32)).astype(jnp.bfloat16)


def gate_both(inner, first, second):
    groups, rows, width = inner.shape
    columns = groups * width
    steps = 4
    per = groups // steps
    flat = pl.BlockSpec((rows, per * width), lambda i: (0, i))
    return pl.pallas_call(
        gate_kernel,
        grid=(steps,),
        in_specs=[pl.BlockSpec((per, rows, width), lambda i: (i, 0, 0)), flat, flat],
        out_specs=[flat, flat],
        out_shape=[jax.ShapeDtypeStruct((rows, columns), jnp.bfloat16)] * 2,
        compiler_params=params(),
        cost_estimate=cost(2 * rows * columns, 10 * rows * columns),
        name="gate_both",
    )(inner, first, second)


def taps_kernel(taps_ref, into_ref, out_ref):
    step = pl.program_id(0)
    part = jnp.dot(
        into_ref[0], taps_ref[...].astype(jnp.bfloat16), preferred_element_type=jnp.float32
    )

    @pl.when(step == 0)
    def _():
        out_ref[...] = part

    @pl.when(step > 0)
    def _():
        out_ref[...] += part


def taps_spectrum(taps, into):
    reach, width = taps.shape
    size = into.shape[1]
    return pl.pallas_call(
        taps_kernel,
        grid=(reach // BLOCK,),
        in_specs=[
            pl.BlockSpec((BLOCK, width), lambda i: (i, 0)),
            pl.BlockSpec((1, size, BLOCK), lambda i: (i, 0, 0)),
        ],
        out_specs=pl.BlockSpec((size, width), lambda i: (0, 0)),
        out_shape=jax.ShapeDtypeStruct((size, width), jnp.float32),
        compiler_params=params(),
        cost_estimate=cost(2 * reach * size * width, 2 * reach * size + 4 * size * width),
        name="taps_spectrum",
    )(taps, into)


def window_ends(lengths_ref):
    first = lengths_ref[0, 0]
    second = first + lengths_ref[0, 1]
    return first, second


def window_of(place, ends):
    return (place >= ends[0]).astype(jnp.int32) + (place >= ends[1]).astype(jnp.int32)


def inside_window(window, base, shape, ends):
    places = base + lax.broadcasted_iota(jnp.int32, shape, 0)
    low = jnp.where(window == 0, 0, jnp.where(window == 1, ends[0], ends[1]))
    high = jnp.where(window == 0, ends[0], jnp.where(window == 1, ends[1], 1 << 30))
    return (places >= low) & (places < high)


def gather_spectra(block, ends, field_ref, into_ref, sums_ref):
    base = block * BLOCK
    field = field_ref[...].astype(jnp.float32)

    def one_window(window, carry):
        mask = inside_window(window, base, field.shape, ends)
        part = jnp.where(mask, field, 0.0).astype(jnp.bfloat16)
        sums_ref[window] += jnp.dot(into_ref[0], part, preferred_element_type=jnp.float32)
        return carry

    lax.fori_loop(window_of(base, ends), window_of(base + BLOCK - 1, ends) + 1, one_window, 0)


def scatter_back(block, ends, field_ref, gain_ref, back_ref, spectra_ref, total_ref, out_ref):
    base = block * BLOCK
    total_ref[...] = gain_ref[...] * field_ref[...].astype(jnp.float32)

    def one_window(window, carry):
        mask = inside_window(window, base, total_ref.shape, ends)
        part = jnp.dot(back_ref[0], spectra_ref[window], preferred_element_type=jnp.float32)
        total_ref[...] += jnp.where(mask, part, 0.0)
        return carry

    lax.fori_loop(window_of(base, ends), window_of(base + BLOCK - 1, ends) + 1, one_window, 0)
    out_ref[...] = total_ref[...].astype(jnp.bfloat16)


def forward_kernel(
    lengths_ref, field_ref, gain_ref, into_ref, back_ref, taps_any, out_ref, saved_any,
    sums_ref, taps_ref, spectra_ref, saved_ref, total_ref, sems,
):
    step = pl.program_id(0)
    blocks = pl.num_programs(0) // 2
    half = sums_ref.shape[1] // 2
    ends = window_ends(lengths_ref)
    taps_copy = pltpu.make_async_copy(taps_any, taps_ref, sems.at[0])
    saved_copy = pltpu.make_async_copy(saved_ref, saved_any, sems.at[1])

    @pl.when(step == 0)
    def _():
        taps_copy.start()
        sums_ref[...] = jnp.zeros_like(sums_ref)

    @pl.when(step < blocks)
    def _():
        gather_spectra(step, ends, field_ref, into_ref, sums_ref)

    @pl.when(step == blocks)
    def _():
        taps_copy.wait()

        def one_chunk(chunk, carry):
            low = pl.ds(pl.multiple_of(chunk * 64, 64), 64)
            high = pl.ds(pl.multiple_of(half + chunk * 64, 64), 64)
            tap_re, tap_im = taps_ref[low], taps_ref[high]
            for window in range(sums_ref.shape[0]):
                re, im = sums_ref[window, low], sums_ref[window, high]
                saved_ref[window, low] = re.astype(jnp.bfloat16)
                saved_ref[window, high] = im.astype(jnp.bfloat16)
                spectra_ref[window, low] = (tap_re * re - tap_im * im).astype(jnp.bfloat16)
                spectra_ref[window, high] = (tap_re * im + tap_im * re).astype(jnp.bfloat16)
            return carry

        lax.fori_loop(0, half // 64, one_chunk, 0)
        saved_copy.start()

    @pl.when(step >= blocks)
    def _():
        scatter_back(
            step - blocks, ends, field_ref, gain_ref, back_ref, spectra_ref, total_ref, out_ref
        )

    @pl.when(step == 2 * blocks - 1)
    def _():
        saved_copy.wait()


def conv_specs(blocks, size, width):
    return [
        pl.BlockSpec(memory_space=pltpu.SMEM),
        pl.BlockSpec((BLOCK, width), lambda i: (lax.rem(i, blocks), 0)),
        pl.BlockSpec((1, width), lambda i: (0, 0)),
        pl.BlockSpec((1, size, BLOCK), lambda i: (jnp.minimum(i, blocks - 1), 0, 0)),
        pl.BlockSpec((1, BLOCK, size), lambda i: (jnp.maximum(i - blocks, 0), 0, 0)),
    ]


def forward_mix(product, taps_spec, gain, lengths, into, back):
    rows, width = product.shape
    blocks, size, _ = into.shape
    windows = lengths.shape[1]
    return pl.pallas_call(
        forward_kernel,
        grid=(2 * blocks,),
        in_specs=conv_specs(blocks, size, width) + [pl.BlockSpec(memory_space=pl.ANY)],
        out_specs=[
            pl.BlockSpec((BLOCK, width), lambda i: (jnp.maximum(i - blocks, 0), 0)),
            pl.BlockSpec(memory_space=pl.ANY),
        ],
        out_shape=[
            jax.ShapeDtypeStruct((rows, width), jnp.bfloat16),
            jax.ShapeDtypeStruct((windows, size, width), jnp.bfloat16),
        ],
        scratch_shapes=[
            pltpu.VMEM((windows, size, width), jnp.float32),
            pltpu.VMEM((size, width), jnp.float32),
            pltpu.VMEM((windows, size, width), jnp.bfloat16),
            pltpu.VMEM((windows, size, width), jnp.bfloat16),
            pltpu.VMEM((BLOCK, width), jnp.float32),
            pltpu.SemaphoreType.DMA((2,)),
        ],
        compiler_params=params(),
        cost_estimate=cost(5 * rows * size * width, 4 * rows * size + 16 * size * width),
        name="forward_mix",
    )(lengths, product, gain, into, back, taps_spec)


def backward_kernel(
    lengths_ref, field_ref, gain_ref, into_ref, back_ref, taps_any, saved_any, out_ref, filter_ref,
    sums_ref, taps_ref, saved_ref, spectra_ref, cross_ref, total_ref, sems,
):
    step = pl.program_id(0)
    blocks = pl.num_programs(0) // 2
    half = sums_ref.shape[1] // 2
    ends = window_ends(lengths_ref)
    taps_copy = pltpu.make_async_copy(taps_any, taps_ref, sems.at[0])
    saved_copy = pltpu.make_async_copy(saved_any, saved_ref, sems.at[1])

    @pl.when(step == 0)
    def _():
        taps_copy.start()
        saved_copy.start()
        sums_ref[...] = jnp.zeros_like(sums_ref)

    @pl.when(step < blocks)
    def _():
        gather_spectra(step, ends, field_ref, into_ref, sums_ref)

    @pl.when(step == blocks)
    def _():
        taps_copy.wait()
        saved_copy.wait()

        def one_chunk(chunk, carry):
            low = pl.ds(pl.multiple_of(chunk * 64, 64), 64)
            high = pl.ds(pl.multiple_of(half + chunk * 64, 64), 64)
            tap_re, tap_im = taps_ref[low], taps_ref[high]
            cross_re = jnp.zeros(tap_re.shape, jnp.float32)
            cross_im = jnp.zeros(tap_re.shape, jnp.float32)
            for window in range(sums_ref.shape[0]):
                re, im = sums_ref[window, low], sums_ref[window, high]
                spectra_ref[window, low] = (tap_re * re + tap_im * im).astype(jnp.bfloat16)
                spectra_ref[window, high] = (tap_re * im - tap_im * re).astype(jnp.bfloat16)
                old_re = saved_ref[window, low].astype(jnp.float32)
                old_im = saved_ref[window, high].astype(jnp.float32)
                cross_re += re * old_re + im * old_im
                cross_im += im * old_re - re * old_im
            cross_ref[low] = cross_re.astype(jnp.bfloat16)
            cross_ref[high] = cross_im.astype(jnp.bfloat16)
            return carry

        lax.fori_loop(0, half // 64, one_chunk, 0)

    @pl.when((step >= blocks) & (step < blocks + blocks // 2))
    def _():
        part = jnp.dot(back_ref[0], cross_ref[...], preferred_element_type=jnp.float32)
        filter_ref[...] = part.astype(jnp.bfloat16)

    @pl.when(step >= blocks)
    def _():
        scatter_back(
            step - blocks, ends, field_ref, gain_ref, back_ref, spectra_ref, total_ref, out_ref
        )


def backward_mix(delta, taps_spec, saved, gain, lengths, into, back):
    rows, width = delta.shape
    blocks, size, _ = into.shape
    windows = lengths.shape[1]
    return pl.pallas_call(
        backward_kernel,
        grid=(2 * blocks,),
        in_specs=conv_specs(blocks, size, width) + [pl.BlockSpec(memory_space=pl.ANY)] * 2,
        out_specs=[
            pl.BlockSpec((BLOCK, width), lambda i: (jnp.maximum(i - blocks, 0), 0)),
            pl.BlockSpec(
                (BLOCK, width), lambda i: (jnp.clip(i - blocks, 0, blocks // 2 - 1), 0)
            ),
        ],
        out_shape=[
            jax.ShapeDtypeStruct((rows, width), jnp.bfloat16),
            jax.ShapeDtypeStruct((rows // 2, width), jnp.bfloat16),
        ],
        scratch_shapes=[
            pltpu.VMEM((windows, size, width), jnp.float32),
            pltpu.VMEM((size, width), jnp.float32),
            pltpu.VMEM((windows, size, width), jnp.bfloat16),
            pltpu.VMEM((windows, size, width), jnp.bfloat16),
            pltpu.VMEM((size, width), jnp.bfloat16),
            pltpu.VMEM((BLOCK, width), jnp.float32),
            pltpu.SemaphoreType.DMA((2,)),
        ],
        compiler_params=params(),
        cost_estimate=cost(6 * rows * size * width, 4 * rows * size + 16 * size * width),
        name="backward_mix",
    )(lengths, delta, gain, into, back, taps_spec, saved)


def swap(pieces):
    return lax.all_to_all(pieces, "ctx", split_axis=0, concat_axis=0, tiled=True)


def shards(queries, key_inputs, value_inputs, cotangent, filter_taps, skip_gain, lengths):
    groups = lax.axis_size("ctx")
    rows = queries.shape[1]
    total = rows * groups
    reach, width = filter_taps.shape
    into, back = transform_tables(total, reach)
    into, back = jnp.asarray(into), jnp.asarray(back)
    gain = skip_gain[None, :]
    product_cols = swap(pair_product(key_inputs[0], value_inputs[0], groups))
    delta_cols = swap(pair_product(cotangent[0], queries[0], groups))
    taps_spec = taps_spectrum(filter_taps, into)
    mixing, saved = forward_mix(
        product_cols.reshape(total, width), taps_spec, gain, lengths, into, back
    )
    mixing_rows = swap(mixing.reshape(groups, rows, width))
    units, filter_local = backward_mix(
        delta_cols.reshape(total, width), taps_spec, saved, gain, lengths, into, back
    )
    units_rows = swap(units.reshape(groups, rows, width))
    filter_grad = lax.psum_scatter(
        filter_local, "dp", scatter_dimension=0, tiled=True
    ).astype(jnp.float32) / lax.axis_size("dp")
    mixed_out, query_grad = gate_both(mixing_rows, queries[0], cotangent[0])
    key_grad, value_grad = gate_both(units_rows, value_inputs[0], key_inputs[0])
    return (mixed_out[None], query_grad[None], key_grad[None], value_grad[None], filter_grad)


def solution(mesh):
    rows_spec = P("dp", "ctx", None)
    in_specs = (rows_spec,) * 4 + (P(None, "ctx"), P("ctx"), P("dp", None))
    out_specs = (rows_spec,) * 4 + (P("dp", "ctx"),)
    return jax.shard_map(shards, mesh=mesh, in_specs=in_specs, out_specs=out_specs, check_vma=False)
```

```python
import math

import jax
import jax.numpy as jnp
import numpy as np
from jax import lax
from jax.experimental import pallas as pl
from jax.experimental.pallas import tpu as pltpu
from jax.sharding import PartitionSpec as P

MIB = 1024 * 1024
LANES = 128
TILE = 256
STRIP = 512
FAR = pl.BlockSpec(memory_space=pltpu.HBM)
SCALARS = pl.BlockSpec(memory_space=pltpu.SMEM)
LOCAL = pl.BlockSpec(memory_space=pltpu.VMEM)


def transform_tables(reach):
    places = np.arange(reach)
    doubled = (2 * np.arange(reach)[:, None] + 1) * places[None, :] % (4 * reach)
    angle = doubled * (math.pi / (2 * reach))
    rows = np.stack([np.cos(angle), -np.sin(angle)], 0)
    rows = rows.reshape(2, 2 * reach // TILE, TILE // 2, reach).transpose(1, 0, 2, 3)
    rows = rows.reshape(2 * reach, reach)
    return rows.astype(jnp.bfloat16), (rows.T / reach).astype(jnp.bfloat16)


def cost(flops, nbytes):
    return pl.CostEstimate(flops=flops, bytes_accessed=nbytes, transcendentals=0)


def far(array):
    return pltpu.with_memory_space_constraint(array, pltpu.HBM)


def near(array):
    return pltpu.with_memory_space_constraint(array, pltpu.VMEM)


def params(mebibytes):
    return pltpu.CompilerParams(vmem_limit_bytes=mebibytes * MIB)


def pair_kernel(left_any, right_any, out_any, left_ref, right_ref, out_ref, sems):
    width = out_ref.shape[2]
    chunks = sems.shape[1]
    per = out_ref.shape[0] // chunks
    loads = []
    for chunk in range(chunks):
        cols = pl.ds(chunk * per * width, per * width)
        for index, (source, held) in enumerate(((left_any, left_ref), (right_any, right_ref))):
            copy = pltpu.make_async_copy(
                source.at[:, cols], held.at[:, cols], sems.at[index, chunk]
            )
            copy.start()
            loads.append(copy)
    stores = []
    for chunk in range(chunks):
        loads[2 * chunk].wait()
        loads[2 * chunk + 1].wait()
        for part in range(chunk * per, (chunk + 1) * per):
            cols = slice(part * width, (part + 1) * width)
            left = left_ref[:, cols].astype(jnp.float32)
            right = right_ref[:, cols].astype(jnp.float32)
            out_ref[part] = (left * right).astype(jnp.bfloat16)
        rows = pl.ds(chunk * per, per)
        copy = pltpu.make_async_copy(out_ref.at[rows], out_any.at[rows], sems.at[2, chunk])
        copy.start()
        stores.append(copy)
    for copy in stores:
        copy.wait()


def pair_product(left, right, groups):
    rows, columns = left.shape
    shape = (groups, rows, columns // groups)
    return pl.pallas_call(
        pair_kernel,
        in_specs=[FAR] * 2,
        out_specs=FAR,
        out_shape=pltpu.HBM(shape, jnp.bfloat16),
        scratch_shapes=[
            pltpu.VMEM((rows, columns), jnp.bfloat16),
            pltpu.VMEM((rows, columns), jnp.bfloat16),
            pltpu.VMEM(shape, jnp.bfloat16),
            pltpu.SemaphoreType.DMA((3, 4)),
        ],
        compiler_params=params(8),
        cost_estimate=cost(rows * columns, 6 * rows * columns),
        name="pair_product",
    )(far(left), far(right))


def gate_kernel(
    inner_any, first_any, second_any, ahead_any, one_any, two_any, ahead_out,
    inner_ref, first_ref, second_ref, one_ref, two_ref, sems, hold_sem,
):
    groups, _, width = inner_ref.shape
    chunks = sems.shape[1]
    per = groups // chunks
    loads, stores = [], []
    for chunk in range(chunks):
        rows = pl.ds(chunk * per, per)
        cols = pl.ds(chunk * per * width, per * width)
        for copy in (
            pltpu.make_async_copy(inner_any.at[rows], inner_ref.at[rows], sems.at[0, chunk]),
            pltpu.make_async_copy(first_any.at[:, cols], first_ref.at[:, cols], sems.at[1, chunk]),
            pltpu.make_async_copy(second_any.at[:, cols], second_ref.at[:, cols], sems.at[2, chunk]),
        ):
            copy.start()
            loads.append(copy)
    copy = pltpu.make_async_copy(ahead_any, ahead_out, hold_sem)
    copy.start()
    stores.append(copy)
    for chunk in range(chunks):
        for copy in loads[3 * chunk : 3 * chunk + 3]:
            copy.wait()
        for part in range(chunk * per, (chunk + 1) * per):
            cols = slice(part * width, (part + 1) * width)
            inner = inner_ref[part].astype(jnp.float32)
            one_ref[:, cols] = (inner * first_ref[:, cols].astype(jnp.float32)).astype(jnp.bfloat16)
            two_ref[:, cols] = (inner * second_ref[:, cols].astype(jnp.float32)).astype(
                jnp.bfloat16
            )
        cols = pl.ds(chunk * per * width, per * width)
        for index, (held, target) in enumerate(((one_ref, one_any), (two_ref, two_any))):
            copy = pltpu.make_async_copy(
                held.at[:, cols], target.at[:, cols], sems.at[3 + index, chunk]
            )
            copy.start()
            stores.append(copy)
    for copy in stores:
        copy.wait()


def gate_both(inner, first, second, ahead):
    groups, rows, width = inner.shape
    columns = groups * width
    held = pltpu.VMEM((rows, columns), jnp.bfloat16)
    return pl.pallas_call(
        gate_kernel,
        in_specs=[pl.BlockSpec(memory_space=pl.ANY)] + [FAR] * 3,
        out_specs=[FAR] * 2 + [LOCAL],
        out_shape=[pltpu.HBM((rows, columns), jnp.bfloat16)] * 2 + [held],
        scratch_shapes=[
            pltpu.VMEM((groups, rows, width), jnp.bfloat16),
            held, held, held, held,
            pltpu.SemaphoreType.DMA((5, 4)),
            pltpu.SemaphoreType.DMA,
        ],
        compiler_params=params(12),
        cost_estimate=cost(2 * rows * columns, 12 * rows * columns),
        name="gate_both",
    )(inner, far(first), far(second), far(ahead))


def last_kernel(
    inner_ref, first_any, second_ref, one_any, two_any, first_ref, one_ref, two_ref, sems
):
    groups, _, width = inner_ref.shape
    chunks = sems.shape[1]
    per = groups // chunks
    loads, stores = [], []
    for chunk in range(chunks):
        cols = pl.ds(chunk * per * width, per * width)
        copy = pltpu.make_async_copy(first_any.at[:, cols], first_ref.at[:, cols], sems.at[2, chunk])
        copy.start()
        loads.append(copy)
    for chunk in range(chunks):
        loads[chunk].wait()
        for part in range(chunk * per, (chunk + 1) * per):
            cols = slice(part * width, (part + 1) * width)
            inner = inner_ref[part].astype(jnp.float32)
            one_ref[:, cols] = (inner * first_ref[:, cols].astype(jnp.float32)).astype(jnp.bfloat16)
            two_ref[:, cols] = (inner * second_ref[:, cols].astype(jnp.float32)).astype(
                jnp.bfloat16
            )
        cols = pl.ds(chunk * per * width, per * width)
        for index, (held, target) in enumerate(((one_ref, one_any), (two_ref, two_any))):
            copy = pltpu.make_async_copy(held.at[:, cols], target.at[:, cols], sems.at[index, chunk])
            copy.start()
            stores.append(copy)
    for copy in stores:
        copy.wait()


def gate_last(inner, first, second):
    groups, rows, width = inner.shape
    columns = groups * width
    held = pltpu.VMEM((rows, columns), jnp.bfloat16)
    return pl.pallas_call(
        last_kernel,
        in_specs=[LOCAL, FAR, LOCAL],
        out_specs=[FAR] * 2,
        out_shape=[pltpu.HBM((rows, columns), jnp.bfloat16)] * 2,
        scratch_shapes=[held, held, held, pltpu.SemaphoreType.DMA((3, 4))],
        compiler_params=params(8),
        cost_estimate=cost(2 * rows * columns, 10 * rows * columns),
        name="gate_last",
    )(near(inner), far(first), near(second))


def taps_kernel(taps_any, into_any, out_any, taps_ref, into_ref, out_ref, sems):
    size = out_ref.shape[0]
    tiles = size // TILE
    first = pltpu.make_async_copy(taps_any, taps_ref, sems.at[0, 0])
    first.start()
    loads, stores = [], []
    for tile in range(tiles):
        rows = pl.ds(tile * TILE, TILE)
        copy = pltpu.make_async_copy(into_any.at[rows], into_ref.at[rows], sems.at[1, tile])
        copy.start()
        loads.append(copy)
    first.wait()
    taps = taps_ref[...].astype(jnp.bfloat16)
    for tile in range(tiles):
        rows = slice(tile * TILE, (tile + 1) * TILE)
        loads[tile].wait()
        part = jnp.dot(into_ref[rows], taps, preferred_element_type=jnp.float32)
        out_ref[rows] = part.astype(jnp.bfloat16)
        rows = pl.ds(tile * TILE, TILE)
        copy = pltpu.make_async_copy(out_ref.at[rows], out_any.at[rows], sems.at[2, tile])
        copy.start()
        stores.append(copy)
    for copy in stores:
        copy.wait()


def taps_spectrum(taps, into):
    reach, width = taps.shape
    size = into.shape[0]
    return pl.pallas_call(
        taps_kernel,
        in_specs=[FAR] * 2,
        out_specs=FAR,
        out_shape=pltpu.HBM((size, width), jnp.bfloat16),
        scratch_shapes=[
            pltpu.VMEM((reach, width), jnp.float32),
            pltpu.VMEM((size, reach), jnp.bfloat16),
            pltpu.VMEM((size, width), jnp.bfloat16),
            pltpu.SemaphoreType.DMA((3, size // TILE)),
        ],
        compiler_params=params(12),
        cost_estimate=cost(2 * reach * size * width, 2 * reach * size + 4 * size * width),
        name="taps_spectrum",
    )(far(taps), far(into))


def window_order(lengths_ref):
    lengths = [lengths_ref[0, window] for window in range(3)]
    starts = [jnp.int32(0), lengths[0], lengths[0] + lengths[1]]
    first = (lengths[0] >= lengths[1]) & (lengths[0] >= lengths[2])
    second = ~first & (lengths[1] >= lengths[2])
    longest = jnp.where(first, 0, jnp.where(second, 1, 2))
    low = jnp.where(longest == 0, 1, 0)
    high = jnp.where(longest == 2, 1, 2)
    pick = lambda values, index: jnp.where(
        index == 0, values[0], jnp.where(index == 1, values[1], values[2])
    )
    swapped = pick(lengths, low) < pick(lengths, high)
    middle = jnp.where(swapped, high, low)
    shortest = jnp.where(swapped, low, high)
    slots = [(pick(starts, index), pick(lengths, index)) for index in (longest, middle, shortest)]
    places = [
        (
            jnp.where(longest == window, 0, jnp.where(middle == window, 1, 2)),
            starts[window],
            lengths[window],
        )
        for window in range(3)
    ]
    return slots, places


def spread(field_ref, wide_ref):
    rows = field_ref.shape[0]
    for half in range(wide_ref.shape[0]):
        lanes = slice(half * LANES, (half + 1) * LANES)
        wide_ref[half, :rows] = field_ref[:, lanes].astype(jnp.float32)


def take_windows(wide_ref, part_ref, slots):
    reach = part_ref.shape[0]
    for slot, (start, length) in enumerate(slots):
        rows = reach // 2 if slot == 2 else reach
        inside = lax.broadcasted_iota(jnp.int32, (rows, LANES), 0) < length
        for half in range(wide_ref.shape[0]):
            lane = (slot * wide_ref.shape[0] + half) * LANES
            part = jnp.where(inside, wide_ref[half, pl.ds(start, rows)], 0.0)
            part_ref[:rows, lane : lane + LANES] = part.astype(jnp.bfloat16)


def transform_rows(into_ref, part_ref, low, width):
    reach = part_ref.shape[0]
    rows = slice(low, low + TILE)
    long = jnp.dot(into_ref[rows], part_ref[:, : 2 * width], preferred_element_type=jnp.float32)
    short = jnp.dot(
        into_ref[rows, : reach // 2],
        part_ref[: reach // 2, 2 * width :],
        preferred_element_type=jnp.float32,
    )
    return long[:, :width], long[:, width:], short


def place_windows(held_ref, wide_ref, places):
    reach = held_ref.shape[2]
    for slot, start, length in places:

        def body(rows):
            for half in range(wide_ref.shape[0]):
                wide_ref[half, pl.ds(start, rows)] = held_ref[slot, half, :rows]

        @pl.when(length > reach // 2)
        def _():
            body(reach)

        @pl.when(length <= reach // 2)
        def _():
            body(reach // 2)


def hold_rows(held_ref, slot, low, part):
    for half in range(held_ref.shape[1]):
        lanes = slice(half * LANES, (half + 1) * LANES)
        held_ref[slot, half, low : low + part.shape[0]] = part[:, lanes]


def finish(field_ref, gain_ref, wide_ref, out_ref, out_any, sem):
    rows = out_ref.shape[0]
    step = rows // sem.shape[0]
    copies = []
    for index in range(sem.shape[0]):
        place = slice(index * step, (index + 1) * step)
        for half in range(wide_ref.shape[0]):
            lanes = slice(half * LANES, (half + 1) * LANES)
            direct = gain_ref[:, lanes] * field_ref[place, lanes].astype(jnp.float32)
            out_ref[place, lanes] = (wide_ref[half, place] + direct).astype(jnp.bfloat16)
        place = pl.ds(index * step, step)
        copy = pltpu.make_async_copy(out_ref.at[place], out_any.at[place], sem.at[index])
        copy.start()
        copies.append(copy)
    for copy in copies:
        copy.wait()


def copy_parts(source, held, sems):
    parts = sems.shape[0]
    step = source.shape[0] // parts
    copies = []
    for part in range(parts):
        rows = pl.ds(part * step, step)
        copies.append(pltpu.make_async_copy(source.at[rows], held.at[rows], sems.at[part]))
    return copies


def begin(copies):
    for copy in copies:
        copy.start()


def finished(copies):
    for copy in copies:
        copy.wait()


def forward_kernel(
    lengths_ref, field_any, gain_ref, into_any, back_any, taps_any, out_any, saved_any,
    field_ref, into_ref, back_ref, taps_ref, out_ref, saved_ref,
    part_ref, spectra_ref, held_ref, wide_ref, sems, load_sems, out_sems,
):
    size, reach = into_ref.shape
    width = taps_ref.shape[1]
    parts = load_sems.shape[1]
    field_copy = pltpu.make_async_copy(field_any, field_ref, sems.at[0])
    back_copy = pltpu.make_async_copy(back_any, back_ref, sems.at[1])
    into_copies = copy_parts(into_any, into_ref, load_sems.at[0])
    taps_copies = copy_parts(taps_any, taps_ref, load_sems.at[1])
    saved_copies = copy_parts(saved_ref, saved_any, load_sems.at[2])
    stages = [list(copies) for copies in zip(into_copies, taps_copies)]
    begin([field_copy] + stages[0])
    slots, places = window_order(lengths_ref)
    field_copy.wait()
    begin(stages[1] + stages[2])
    spread(field_ref, wide_ref)
    take_windows(wide_ref, part_ref, slots)
    for low in range(0, size, TILE):
        part, start = divmod(low * parts, size)
        if start == 0:
            finished(stages[part])
            begin({0: stages[3], 1: [back_copy]}.get(part, []))
        mid, high = low + TILE // 2, low + TILE
        tap_re = taps_ref[low:mid].astype(jnp.float32)
        tap_im = taps_ref[mid:high].astype(jnp.float32)
        for slot, both in enumerate(transform_rows(into_ref, part_ref, low, width)):
            lanes = slice(slot * width, (slot + 1) * width)
            re, im = both[: TILE // 2], both[TILE // 2 :]
            saved_ref[low:high, lanes] = both.astype(jnp.bfloat16)
            spectra_ref[low:mid, lanes] = (tap_re * re - tap_im * im).astype(jnp.bfloat16)
            spectra_ref[mid:high, lanes] = (tap_re * im + tap_im * re).astype(jnp.bfloat16)
        if start + TILE * parts == size:
            begin([saved_copies[part]])
    back_copy.wait()
    for low in range(0, reach, STRIP):
        long = jnp.dot(
            back_ref[low : low + STRIP],
            spectra_ref[:, : 2 * width],
            preferred_element_type=jnp.float32,
        )
        hold_rows(held_ref, 0, low, long[:, :width])
        hold_rows(held_ref, 1, low, long[:, width:])
    short = jnp.dot(
        back_ref[: reach // 2], spectra_ref[:, 2 * width :], preferred_element_type=jnp.float32
    )
    hold_rows(held_ref, 2, 0, short)
    place_windows(held_ref, wide_ref, places)
    finish(field_ref, gain_ref, wide_ref, out_ref, out_any, out_sems)
    finished(saved_copies)


def forward_mix(product, taps_spec, gain, lengths, into, back):
    rows, width = product.shape
    size, reach = into.shape
    windows = lengths.shape[1]
    return pl.pallas_call(
        forward_kernel,
        in_specs=[SCALARS, FAR, LOCAL, FAR, FAR, FAR],
        out_specs=[FAR] * 2,
        out_shape=[
            pltpu.HBM((rows, width), jnp.bfloat16),
            pltpu.HBM((size, windows * width), jnp.bfloat16),
        ],
        scratch_shapes=[
            pltpu.VMEM((rows, width), jnp.bfloat16),
            pltpu.VMEM((size, reach), jnp.bfloat16),
            pltpu.VMEM((reach, size), jnp.bfloat16),
            pltpu.VMEM((size, width), jnp.bfloat16),
            pltpu.VMEM((rows, width), jnp.bfloat16),
            pltpu.VMEM((size, windows * width), jnp.bfloat16),
            pltpu.VMEM((reach, windows * width), jnp.bfloat16),
            pltpu.VMEM((size, windows * width), jnp.bfloat16),
            pltpu.VMEM((windows, width // LANES, reach, LANES), jnp.float32),
            pltpu.VMEM((width // LANES, rows + reach // 2, LANES), jnp.float32),
            pltpu.SemaphoreType.DMA((2,)),
            pltpu.SemaphoreType.DMA((3, 4)),
            pltpu.SemaphoreType.DMA((4,)),
        ],
        compiler_params=params(40),
        cost_estimate=cost(6 * rows * size * width, 4 * rows * size + 16 * size * width),
        name="forward_mix",
    )(lengths, far(product), gain, far(into), far(back), far(taps_spec))


def backward_kernel(
    lengths_ref, place_ref, field_any, gain_ref, into_any, back_any, taps_any, saved_any,
    out_any, kept_any, away_any,
    field_ref, into_ref, back_ref, taps_ref, out_ref, saved_ref, filter_ref,
    part_ref, spectra_ref, held_ref, wide_ref, sems, load_sems, filter_sems, out_sems,
):
    size, reach = into_ref.shape
    width = taps_ref.shape[1]
    parts = load_sems.shape[1]
    field_copy = pltpu.make_async_copy(field_any, field_ref, sems.at[0])
    back_copy = pltpu.make_async_copy(back_any, back_ref, sems.at[1])
    into_copies = copy_parts(into_any, into_ref, load_sems.at[0])
    taps_copies = copy_parts(taps_any, taps_ref, load_sems.at[1])
    saved_copies = copy_parts(saved_any, saved_ref, load_sems.at[2])
    stages = [list(copies) for copies in zip(into_copies, taps_copies, saved_copies)]
    begin([field_copy] + stages[0])
    slots, places = window_order(lengths_ref)
    field_copy.wait()
    begin(stages[1] + stages[2])
    spread(field_ref, wide_ref)
    take_windows(wide_ref, part_ref, slots)
    for low in range(0, size, TILE):
        part, start = divmod(low * parts, size)
        if start == 0:
            finished(stages[part])
            begin({0: stages[3], 1: [back_copy]}.get(part, []))
        mid, high = low + TILE // 2, low + TILE
        tap_re = taps_ref[low:mid].astype(jnp.float32)
        tap_im = taps_ref[mid:high].astype(jnp.float32)
        cross_re, cross_im = 0.0, 0.0
        for slot, both in enumerate(transform_rows(into_ref, part_ref, low, width)):
            lanes = slice(slot * width, (slot + 1) * width)
            re, im = both[: TILE // 2], both[TILE // 2 :]
            spectra_ref[low:mid, lanes] = (tap_re * re + tap_im * im).astype(jnp.bfloat16)
            spectra_ref[mid:high, lanes] = (tap_re * im - tap_im * re).astype(jnp.bfloat16)
            old_re = saved_ref[low:mid, lanes].astype(jnp.float32)
            old_im = saved_ref[mid:high, lanes].astype(jnp.float32)
            cross_re += re * old_re + im * old_im
            cross_im += im * old_re - re * old_im
        spectra_ref[low:mid, 3 * width :] = cross_re.astype(jnp.bfloat16)
        spectra_ref[mid:high, 3 * width :] = cross_im.astype(jnp.bfloat16)
    back_copy.wait()
    for low in range(0, reach, STRIP):
        rows = slice(low, low + STRIP)
        if low < reach // 2:
            short = jnp.dot(
                back_ref[rows], spectra_ref[:, 2 * width :], preferred_element_type=jnp.float32
            )
            hold_rows(held_ref, 2, low, short[:, :width])
            terms = short[:, width:]
        else:
            terms = jnp.dot(
                back_ref[rows], spectra_ref[:, 3 * width :], preferred_element_type=jnp.float32
            )
        filter_ref[rows] = terms.astype(jnp.bfloat16)

    count, height, _ = kept_any.shape
    core, chip = place_ref[0] % 2, place_ref[0] // 2

    def each_block(act):
        for block in range(2 * count):
            rows = pl.ds(block * height, height)
            for same, target in ((0, kept_any), (1, away_any)):

                @pl.when((core + block) % 2 == same)
                def _():
                    act(
                        pltpu.make_async_copy(
                            filter_ref.at[rows], target.at[(block // 2) ^ chip],
                            filter_sems.at[block],
                        )
                    )

    each_block(lambda copy: copy.start())
    for low in range(0, reach, STRIP):
        long = jnp.dot(
            back_ref[low : low + STRIP],
            spectra_ref[:, : 2 * width],
            preferred_element_type=jnp.float32,
        )
        hold_rows(held_ref, 0, low, long[:, :width])
        hold_rows(held_ref, 1, low, long[:, width:])
    place_windows(held_ref, wide_ref, places)
    finish(field_ref, gain_ref, wide_ref, out_ref, out_any, out_sems)
    each_block(lambda copy: copy.wait())


def backward_mix(delta, taps_spec, saved, gain, lengths, place, into, back, slices):
    rows, width = delta.shape
    size, reach = into.shape
    windows = lengths.shape[1]
    blocks = pltpu.HBM((slices // 2, reach // slices, width), jnp.bfloat16)
    return pl.pallas_call(
        backward_kernel,
        in_specs=[SCALARS, SCALARS, FAR, LOCAL] + [FAR] * 4,
        out_specs=[FAR] * 3,
        out_shape=[pltpu.HBM((rows, width), jnp.bfloat16), blocks, blocks],
        scratch_shapes=[
            pltpu.VMEM((rows, width), jnp.bfloat16),
            pltpu.VMEM((size, reach), jnp.bfloat16),
            pltpu.VMEM((reach, size), jnp.bfloat16),
            pltpu.VMEM((size, width), jnp.bfloat16),
            pltpu.VMEM((rows, width), jnp.bfloat16),
            pltpu.VMEM((size, windows * width), jnp.bfloat16),
            pltpu.VMEM((reach, width), jnp.bfloat16),
            pltpu.VMEM((reach, windows * width), jnp.bfloat16),
            pltpu.VMEM((size, (windows + 1) * width), jnp.bfloat16),
            pltpu.VMEM((windows, width // LANES, reach, LANES), jnp.float32),
            pltpu.VMEM((width // LANES, rows + reach // 2, LANES), jnp.float32),
            pltpu.SemaphoreType.DMA((2,)),
            pltpu.SemaphoreType.DMA((3, 4)),
            pltpu.SemaphoreType.DMA((slices,)),
            pltpu.SemaphoreType.DMA((4,)),
        ],
        compiler_params=params(40),
        cost_estimate=cost(7 * rows * size * width, 4 * rows * size + 16 * size * width),
        name="backward_mix",
    )(
        lengths, place, far(delta), gain, far(into), far(back), far(taps_spec), far(saved)
    )


def total_kernel(own_ref, *refs):
    total = own_ref[...]
    for come_ref in refs[:-1]:
        total = total + come_ref[...].astype(jnp.float32)
    refs[-1][...] = total * (1.0 / (2 * len(refs)))


def total_blocks(own, come):
    return pl.pallas_call(
        total_kernel,
        in_specs=[LOCAL] * (1 + len(come)),
        out_specs=LOCAL,
        out_shape=jax.ShapeDtypeStruct(own.shape, jnp.float32),
        compiler_params=params(4),
        name="total_blocks",
    )(own, *come)


def merge_kernel(kept_ref, come_ref, own_ref, *sent_refs):
    for slot in range(kept_ref.shape[0]):
        block = kept_ref[slot].astype(jnp.float32) + come_ref[slot].astype(jnp.float32)
        if slot == 0:
            own_ref[...] = block
        else:
            sent_refs[slot - 1][...] = block.astype(jnp.bfloat16)


def merge_blocks(kept, come):
    slots, height, width = kept.shape
    return pl.pallas_call(
        merge_kernel,
        in_specs=[LOCAL] * 2,
        out_specs=[LOCAL] * slots,
        out_shape=[jax.ShapeDtypeStruct((height, width), jnp.float32)]
        + [jax.ShapeDtypeStruct((height, width), jnp.bfloat16)] * (slots - 1),
        compiler_params=params(4),
        name="merge_blocks",
    )(kept, come)


def swap(pieces):
    return lax.all_to_all(pieces, "ctx", split_axis=0, concat_axis=0, tiled=True)


def from_core(away):
    count = lax.axis_size("dp")
    return lax.ppermute(away, "dp", [(i, i ^ 1) for i in range(count)])


def from_chips(blocks):
    count = lax.axis_size("dp")
    return [
        lax.ppermute(block, "dp", [(i, i ^ (2 * step)) for i in range(count)])
        for step, block in enumerate(blocks, 1)
    ]


def shards(queries, key_inputs, value_inputs, cotangent, filter_taps, skip_gain, lengths):
    groups = lax.axis_size("ctx")
    slices = lax.axis_size("dp")
    rows = queries.shape[1]
    total = rows * groups
    reach, width = filter_taps.shape
    into, back = transform_tables(reach)
    into, back = jnp.asarray(into), jnp.asarray(back)
    gain = skip_gain[None, :]
    place = lax.axis_index("dp").astype(jnp.int32).reshape(1)
    product = pair_product(key_inputs[0], value_inputs[0], groups)
    product_cols = swap(product)
    filter_taps, product = lax.optimization_barrier((filter_taps, product))
    taps_spec = taps_spectrum(filter_taps, into)
    delta = pair_product(cotangent[0], queries[0], groups)
    delta, taps_spec = lax.optimization_barrier((delta, taps_spec))
    delta_cols = swap(delta)
    mixing, saved = forward_mix(
        product_cols.reshape(total, width), taps_spec, gain, lengths, into, back
    )
    mixing_rows = swap(mixing.reshape(groups, rows, width))
    units, kept, away = backward_mix(
        delta_cols.reshape(total, width), taps_spec, saved, gain, lengths, place, into, back, slices
    )
    units_rows = swap(units.reshape(groups, rows, width))
    own, *sent = merge_blocks(kept, from_core(away))
    came = from_chips(sent)
    own, mixing_rows = lax.optimization_barrier((own, mixing_rows))
    mixed_out, query_grad, key_near = gate_both(
        mixing_rows, queries[0], cotangent[0], key_inputs[0]
    )
    *came, mixed_out = lax.optimization_barrier((*came, mixed_out))
    filter_grad = total_blocks(own, came)
    key_grad, value_grad = gate_last(units_rows, value_inputs[0], key_near)
    return (mixed_out[None], query_grad[None], key_grad[None], value_grad[None], filter_grad)


def solution(mesh):
    rows_spec = P("dp", "ctx", None)
    in_specs = (rows_spec,) * 4 + (P(None, "ctx"), P("ctx"), P("dp", None))
    out_specs = (rows_spec,) * 4 + (P("dp", "ctx"),)
    return jax.shard_map(shards, mesh=mesh, in_specs=in_specs, out_specs=out_specs, check_vma=False)
```

```python
import math

import jax
import jax.numpy as jnp
import numpy as np
from jax import lax
from jax.experimental import pallas as pl
from jax.experimental.pallas import tpu as pltpu
from jax.sharding import PartitionSpec as P

MIB = 1024 * 1024
LANES = 128
TILE = 256
STRIP = 512
FAR = pl.BlockSpec(memory_space=pltpu.HBM)
SCALARS = pl.BlockSpec(memory_space=pltpu.SMEM)
LOCAL = pl.BlockSpec(memory_space=pltpu.VMEM)


def transform_tables(reach):
    places = np.arange(reach)
    doubled = (2 * np.arange(reach)[:, None] + 1) * places[None, :] % (4 * reach)
    angle = doubled * (math.pi / (2 * reach))
    rows = np.stack([np.cos(angle), -np.sin(angle)], 0)
    rows = rows.reshape(2, 2 * reach // TILE, TILE // 2, reach).transpose(1, 0, 2, 3)
    rows = rows.reshape(2 * reach, reach)
    return rows.astype(jnp.bfloat16), (rows.T / reach).astype(jnp.bfloat16)


def cost(flops, nbytes):
    return pl.CostEstimate(flops=flops, bytes_accessed=nbytes, transcendentals=0)


def far(array):
    return pltpu.with_memory_space_constraint(array, pltpu.HBM)


def near(array):
    return pltpu.with_memory_space_constraint(array, pltpu.VMEM)


def params(mebibytes):
    return pltpu.CompilerParams(vmem_limit_bytes=mebibytes * MIB)


def pair_kernel(left_any, right_any, out_any, left_ref, right_ref, out_ref, sems):
    width = out_ref.shape[2]
    chunks = sems.shape[1]
    per = out_ref.shape[0] // chunks
    loads = []
    for chunk in range(chunks):
        cols = pl.ds(chunk * per * width, per * width)
        for index, (source, held) in enumerate(((left_any, left_ref), (right_any, right_ref))):
            copy = pltpu.make_async_copy(
                source.at[:, cols], held.at[:, cols], sems.at[index, chunk]
            )
            copy.start()
            loads.append(copy)
    stores = []
    for chunk in range(chunks):
        loads[2 * chunk].wait()
        loads[2 * chunk + 1].wait()
        for part in range(chunk * per, (chunk + 1) * per):
            cols = slice(part * width, (part + 1) * width)
            left = left_ref[:, cols].astype(jnp.float32)
            right = right_ref[:, cols].astype(jnp.float32)
            out_ref[part] = (left * right).astype(jnp.bfloat16)
        rows = pl.ds(chunk * per, per)
        copy = pltpu.make_async_copy(out_ref.at[rows], out_any.at[rows], sems.at[2, chunk])
        copy.start()
        stores.append(copy)
    for copy in stores:
        copy.wait()


def gate_kernel(
    inner_any, first_any, second_any, ahead_any, one_any, two_any, ahead_out,
    inner_ref, first_ref, second_ref, one_ref, two_ref, sems, hold_sem,
):
    groups, _, width = inner_ref.shape
    chunks = sems.shape[1]
    per = groups // chunks
    loads, stores = [], []
    for chunk in range(chunks):
        rows = pl.ds(chunk * per, per)
        cols = pl.ds(chunk * per * width, per * width)
        for copy in (
            pltpu.make_async_copy(inner_any.at[rows], inner_ref.at[rows], sems.at[0, chunk]),
            pltpu.make_async_copy(first_any.at[:, cols], first_ref.at[:, cols], sems.at[1, chunk]),
            pltpu.make_async_copy(second_any.at[:, cols], second_ref.at[:, cols], sems.at[2, chunk]),
        ):
            copy.start()
            loads.append(copy)
    copy = pltpu.make_async_copy(ahead_any, ahead_out, hold_sem)
    copy.start()
    stores.append(copy)
    for chunk in range(chunks):
        for copy in loads[3 * chunk : 3 * chunk + 3]:
            copy.wait()
        for part in range(chunk * per, (chunk + 1) * per):
            cols = slice(part * width, (part + 1) * width)
            inner = inner_ref[part].astype(jnp.float32)
            one_ref[:, cols] = (inner * first_ref[:, cols].astype(jnp.float32)).astype(jnp.bfloat16)
            two_ref[:, cols] = (inner * second_ref[:, cols].astype(jnp.float32)).astype(
                jnp.bfloat16
            )
        cols = pl.ds(chunk * per * width, per * width)
        for index, (held, target) in enumerate(((one_ref, one_any), (two_ref, two_any))):
            copy = pltpu.make_async_copy(
                held.at[:, cols], target.at[:, cols], sems.at[3 + index, chunk]
            )
            copy.start()
            stores.append(copy)
    for copy in stores:
        copy.wait()


def gate_both(inner, first, second, ahead):
    groups, rows, width = inner.shape
    columns = groups * width
    held = pltpu.VMEM((rows, columns), jnp.bfloat16)
    return pl.pallas_call(
        gate_kernel,
        in_specs=[pl.BlockSpec(memory_space=pl.ANY)] + [FAR] * 3,
        out_specs=[FAR] * 2 + [LOCAL],
        out_shape=[pltpu.HBM((rows, columns), jnp.bfloat16)] * 2 + [held],
        scratch_shapes=[
            pltpu.VMEM((groups, rows, width), jnp.bfloat16),
            held, held, held, held,
            pltpu.SemaphoreType.DMA((5, 4)),
            pltpu.SemaphoreType.DMA,
        ],
        compiler_params=params(12),
        cost_estimate=cost(2 * rows * columns, 12 * rows * columns),
        name="gate_both",
    )(inner, far(first), far(second), far(ahead))


def last_kernel(
    inner_ref, first_any, second_ref, one_any, two_any, first_ref, one_ref, two_ref, sems
):
    groups, _, width = inner_ref.shape
    chunks = sems.shape[1]
    per = groups // chunks
    loads, stores = [], []
    for chunk in range(chunks):
        cols = pl.ds(chunk * per * width, per * width)
        copy = pltpu.make_async_copy(first_any.at[:, cols], first_ref.at[:, cols], sems.at[2, chunk])
        copy.start()
        loads.append(copy)
    for chunk in range(chunks):
        loads[chunk].wait()
        for part in range(chunk * per, (chunk + 1) * per):
            cols = slice(part * width, (part + 1) * width)
            inner = inner_ref[part].astype(jnp.float32)
            one_ref[:, cols] = (inner * first_ref[:, cols].astype(jnp.float32)).astype(jnp.bfloat16)
            two_ref[:, cols] = (inner * second_ref[:, cols].astype(jnp.float32)).astype(
                jnp.bfloat16
            )
        cols = pl.ds(chunk * per * width, per * width)
        for index, (held, target) in enumerate(((one_ref, one_any), (two_ref, two_any))):
            copy = pltpu.make_async_copy(held.at[:, cols], target.at[:, cols], sems.at[index, chunk])
            copy.start()
            stores.append(copy)
    for copy in stores:
        copy.wait()


def gate_last(inner, first, second):
    groups, rows, width = inner.shape
    columns = groups * width
    held = pltpu.VMEM((rows, columns), jnp.bfloat16)
    return pl.pallas_call(
        last_kernel,
        in_specs=[LOCAL, FAR, LOCAL],
        out_specs=[FAR] * 2,
        out_shape=[pltpu.HBM((rows, columns), jnp.bfloat16)] * 2,
        scratch_shapes=[held, held, held, pltpu.SemaphoreType.DMA((3, 4))],
        compiler_params=params(8),
        cost_estimate=cost(2 * rows * columns, 10 * rows * columns),
        name="gate_last",
    )(near(inner), far(first), near(second))


def taps_kernel(taps_any, into_any, out_any, taps_ref, into_ref, out_ref, sems):
    size = out_ref.shape[0]
    tiles = size // TILE
    first = pltpu.make_async_copy(taps_any, taps_ref, sems.at[0, 0])
    first.start()
    loads, stores = [], []
    for tile in range(tiles):
        rows = pl.ds(tile * TILE, TILE)
        copy = pltpu.make_async_copy(into_any.at[rows], into_ref.at[rows], sems.at[1, tile])
        copy.start()
        loads.append(copy)
    first.wait()
    taps = taps_ref[...].astype(jnp.bfloat16)
    for tile in range(tiles):
        rows = slice(tile * TILE, (tile + 1) * TILE)
        loads[tile].wait()
        part = jnp.dot(into_ref[rows], taps, preferred_element_type=jnp.float32)
        out_ref[rows] = part.astype(jnp.bfloat16)
        rows = pl.ds(tile * TILE, TILE)
        copy = pltpu.make_async_copy(out_ref.at[rows], out_any.at[rows], sems.at[2, tile])
        copy.start()
        stores.append(copy)
    for copy in stores:
        copy.wait()


def opening_kernel(
    key_any, value_any, cot_any, query_any, taps_any, into_any,
    product_any, delta_any, spectrum_any,
    left_ref, right_ref, pair_ref, pair_sems, taps_ref, into_ref, spectrum_ref, taps_sems,
):
    pair = (left_ref, right_ref, pair_ref, pair_sems)
    pair_kernel(key_any, value_any, product_any, *pair)

    @pl.when(lax.axis_index("dp") % 2 == 1)
    def _():
        pair_kernel(cot_any, query_any, delta_any, *pair)
        taps_kernel(taps_any, into_any, spectrum_any, taps_ref, into_ref, spectrum_ref, taps_sems)


def second_kernel(
    cot_any, query_any, taps_any, into_any, _, __, delta_any, spectrum_any,
    left_ref, right_ref, pair_ref, pair_sems, taps_ref, into_ref, spectrum_ref, taps_sems,
):
    @pl.when(lax.axis_index("dp") % 2 == 0)
    def _():
        pair_kernel(
            cot_any, query_any, delta_any, left_ref, right_ref, pair_ref, pair_sems
        )
        taps_kernel(taps_any, into_any, spectrum_any, taps_ref, into_ref, spectrum_ref, taps_sems)


def opening_scratch(rows, columns, groups, reach, size, width):
    return [
        pltpu.VMEM((rows, columns), jnp.bfloat16),
        pltpu.VMEM((rows, columns), jnp.bfloat16),
        pltpu.VMEM((groups, rows, columns // groups), jnp.bfloat16),
        pltpu.SemaphoreType.DMA((3, 4)),
        pltpu.VMEM((reach, width), jnp.float32),
        pltpu.VMEM((size, reach), jnp.bfloat16),
        pltpu.VMEM((size, width), jnp.bfloat16),
        pltpu.SemaphoreType.DMA((3, size // TILE)),
    ]


def opening(key, value, cotangent, queries, taps, into, groups):
    rows, columns = key.shape
    reach, width = taps.shape
    size = into.shape[0]
    pieces = pltpu.HBM((groups, rows, columns // groups), jnp.bfloat16)
    return pl.pallas_call(
        opening_kernel,
        in_specs=[FAR] * 6,
        out_specs=[FAR] * 3,
        out_shape=[pieces, pieces, pltpu.HBM((size, width), jnp.bfloat16)],
        scratch_shapes=opening_scratch(rows, columns, groups, reach, size, width),
        compiler_params=params(20),
        cost_estimate=cost(rows * columns, 6 * rows * columns),
        name="opening",
    )(far(key), far(value), far(cotangent), far(queries), far(taps), far(into))


def second(cotangent, queries, taps, into, delta, spectrum):
    rows, columns = queries.shape
    reach, width = taps.shape
    size = into.shape[0]
    groups = delta.shape[0]
    return pl.pallas_call(
        second_kernel,
        in_specs=[FAR] * 6,
        out_specs=[FAR] * 2,
        out_shape=[pltpu.HBM(delta.shape, delta.dtype), pltpu.HBM(spectrum.shape, spectrum.dtype)],
        input_output_aliases={4: 0, 5: 1},
        scratch_shapes=opening_scratch(rows, columns, groups, reach, size, width),
        compiler_params=params(20),
        cost_estimate=cost(2 * reach * size * width, 2 * reach * size + 4 * size * width),
        name="second",
    )(far(cotangent), far(queries), far(taps), far(into), far(delta), far(spectrum))


def window_order(lengths_ref):
    lengths = [lengths_ref[0, window] for window in range(3)]
    starts = [jnp.int32(0), lengths[0], lengths[0] + lengths[1]]
    first = (lengths[0] >= lengths[1]) & (lengths[0] >= lengths[2])
    second = ~first & (lengths[1] >= lengths[2])
    longest = jnp.where(first, 0, jnp.where(second, 1, 2))
    low = jnp.where(longest == 0, 1, 0)
    high = jnp.where(longest == 2, 1, 2)
    pick = lambda values, index: jnp.where(
        index == 0, values[0], jnp.where(index == 1, values[1], values[2])
    )
    swapped = pick(lengths, low) < pick(lengths, high)
    middle = jnp.where(swapped, high, low)
    shortest = jnp.where(swapped, low, high)
    slots = [(pick(starts, index), pick(lengths, index)) for index in (longest, middle, shortest)]
    places = [
        (
            jnp.where(longest == window, 0, jnp.where(middle == window, 1, 2)),
            starts[window],
            lengths[window],
        )
        for window in range(3)
    ]
    return slots, places


def spread(field_ref, wide_ref, copies):
    step = field_ref.shape[0] // len(copies)
    for part, copy in enumerate(copies):
        rows = slice(part * step, (part + 1) * step)
        copy.wait()
        for half in range(wide_ref.shape[0]):
            lanes = slice(half * LANES, (half + 1) * LANES)
            wide_ref[half, rows] = field_ref[rows, lanes].astype(jnp.float32)


def take_windows(wide_ref, part_ref, slots):
    reach = part_ref.shape[0]
    for slot, (start, length) in enumerate(slots):
        rows = reach // 2 if slot == 2 else reach
        inside = lax.broadcasted_iota(jnp.int32, (rows, LANES), 0) < length
        for half in range(wide_ref.shape[0]):
            lane = (slot * wide_ref.shape[0] + half) * LANES
            part = wide_ref[half, pl.ds(start, rows)]
            if slot > 0:
                part = jnp.where(inside, part, 0.0)
            part_ref[:rows, lane : lane + LANES] = part.astype(jnp.bfloat16)


def transform_rows(into_ref, part_ref, low, width):
    reach = part_ref.shape[0]
    rows = slice(low, low + TILE)
    long = jnp.dot(into_ref[rows], part_ref[:, : 2 * width], preferred_element_type=jnp.float32)
    short = jnp.dot(
        into_ref[rows, : reach // 2],
        part_ref[: reach // 2, 2 * width :],
        preferred_element_type=jnp.float32,
    )
    return long[:, :width], long[:, width:], short


def place_windows(held_ref, wide_ref, places):
    reach = held_ref.shape[2]
    for slot, start, length in places:

        def body(rows):
            for half in range(wide_ref.shape[0]):
                wide_ref[half, pl.ds(start, rows)] = held_ref[slot, half, :rows]

        @pl.when(length > reach // 2)
        def _():
            body(reach)

        @pl.when(length <= reach // 2)
        def _():
            body(reach // 2)


def hold_rows(held_ref, slot, low, part):
    for half in range(held_ref.shape[1]):
        lanes = slice(half * LANES, (half + 1) * LANES)
        held_ref[slot, half, low : low + part.shape[0]] = part[:, lanes]


def finish(field_ref, gain_ref, wide_ref, out_ref, out_any, sem):
    rows = out_ref.shape[0]
    step = rows // sem.shape[0]
    copies = []
    for index in range(sem.shape[0]):
        place = slice(index * step, (index + 1) * step)
        for half in range(wide_ref.shape[0]):
            lanes = slice(half * LANES, (half + 1) * LANES)
            direct = gain_ref[:, lanes] * field_ref[place, lanes].astype(jnp.float32)
            out_ref[place, lanes] = (wide_ref[half, place] + direct).astype(jnp.bfloat16)
        place = pl.ds(index * step, step)
        copy = pltpu.make_async_copy(out_ref.at[place], out_any.at[place], sem.at[index])
        copy.start()
        copies.append(copy)
    for copy in copies:
        copy.wait()


def copy_parts(source, held, sems):
    parts = sems.shape[0]
    step = source.shape[0] // parts
    copies = []
    for part in range(parts):
        rows = pl.ds(part * step, step)
        copies.append(pltpu.make_async_copy(source.at[rows], held.at[rows], sems.at[part]))
    return copies


def begin(copies):
    for copy in copies:
        copy.start()


def finished(copies):
    for copy in copies:
        copy.wait()


def forward_kernel(
    lengths_ref, field_any, gain_ref, into_any, back_any, taps_any, out_any, saved_any,
    field_ref, into_ref, back_ref, taps_ref, out_ref, saved_ref,
    part_ref, spectra_ref, held_ref, wide_ref, field_sems, back_sem, load_sems, out_sems,
):
    size, reach = into_ref.shape
    width = taps_ref.shape[1]
    parts = load_sems.shape[1]
    field_copies = copy_parts(field_any, field_ref, field_sems)
    back_copy = pltpu.make_async_copy(back_any, back_ref, back_sem)
    into_copies = copy_parts(into_any, into_ref, load_sems.at[0])
    taps_copies = copy_parts(taps_any, taps_ref, load_sems.at[1])
    saved_copies = copy_parts(saved_ref, saved_any, load_sems.at[2])
    stages = [list(copies) for copies in zip(into_copies, taps_copies)]
    begin(field_copies + stages[0])
    slots, places = window_order(lengths_ref)
    spread(field_ref, wide_ref, field_copies)
    begin(stages[1] + stages[2])
    take_windows(wide_ref, part_ref, slots)
    for low in range(0, size, TILE):
        part, start = divmod(low * parts, size)
        if start == 0:
            finished(stages[part])
            begin({0: stages[3], 1: [back_copy]}.get(part, []))
        mid, high = low + TILE // 2, low + TILE
        tap_re = taps_ref[low:mid].astype(jnp.float32)
        tap_im = taps_ref[mid:high].astype(jnp.float32)
        for slot, both in enumerate(transform_rows(into_ref, part_ref, low, width)):
            lanes = slice(slot * width, (slot + 1) * width)
            re, im = both[: TILE // 2], both[TILE // 2 :]
            saved_ref[low:high, lanes] = both.astype(jnp.bfloat16)
            spectra_ref[low:mid, lanes] = (tap_re * re - tap_im * im).astype(jnp.bfloat16)
            spectra_ref[mid:high, lanes] = (tap_re * im + tap_im * re).astype(jnp.bfloat16)
        if start + TILE * parts == size:
            begin([saved_copies[part]])
    back_copy.wait()
    for low in range(0, reach, STRIP):
        long = jnp.dot(
            back_ref[low : low + STRIP],
            spectra_ref[:, : 2 * width],
            preferred_element_type=jnp.float32,
        )
        hold_rows(held_ref, 0, low, long[:, :width])
        hold_rows(held_ref, 1, low, long[:, width:])
    short = jnp.dot(
        back_ref[: reach // 2], spectra_ref[:, 2 * width :], preferred_element_type=jnp.float32
    )
    hold_rows(held_ref, 2, 0, short)
    place_windows(held_ref, wide_ref, places)
    finish(field_ref, gain_ref, wide_ref, out_ref, out_any, out_sems)
    finished(saved_copies)


def forward_mix(product, taps_spec, gain, lengths, into, back):
    rows, width = product.shape
    size, reach = into.shape
    windows = lengths.shape[1]
    return pl.pallas_call(
        forward_kernel,
        in_specs=[SCALARS, FAR, LOCAL, FAR, FAR, FAR],
        out_specs=[FAR] * 2,
        out_shape=[
            pltpu.HBM((rows, width), jnp.bfloat16),
            pltpu.HBM((size, windows * width), jnp.bfloat16),
        ],
        scratch_shapes=[
            pltpu.VMEM((rows, width), jnp.bfloat16),
            pltpu.VMEM((size, reach), jnp.bfloat16),
            pltpu.VMEM((reach, size), jnp.bfloat16),
            pltpu.VMEM((size, width), jnp.bfloat16),
            pltpu.VMEM((rows, width), jnp.bfloat16),
            pltpu.VMEM((size, windows * width), jnp.bfloat16),
            pltpu.VMEM((reach, windows * width), jnp.bfloat16),
            pltpu.VMEM((size, windows * width), jnp.bfloat16),
            pltpu.VMEM((windows, width // LANES, reach, LANES), jnp.float32),
            pltpu.VMEM((width // LANES, rows + reach // 2, LANES), jnp.float32),
            pltpu.SemaphoreType.DMA((4,)),
            pltpu.SemaphoreType.DMA,
            pltpu.SemaphoreType.DMA((3, 4)),
            pltpu.SemaphoreType.DMA((4,)),
        ],
        compiler_params=params(40),
        cost_estimate=cost(6 * rows * size * width, 4 * rows * size + 16 * size * width),
        name="forward_mix",
    )(lengths, far(product), gain, far(into), far(back), far(taps_spec))


def backward_kernel(
    lengths_ref, field_any, gain_ref, into_any, back_any, taps_any, saved_any,
    out_any, own_any, one_any, two_any, three_any,
    field_ref, into_ref, back_ref, taps_ref, out_ref, saved_ref, filter_ref,
    part_ref, spectra_ref, held_ref, wide_ref, field_sems, back_sem, load_sems, filter_sems, out_sems,
):
    size, reach = into_ref.shape
    width = taps_ref.shape[1]
    parts = load_sems.shape[1]
    field_copies = copy_parts(field_any, field_ref, field_sems)
    back_copy = pltpu.make_async_copy(back_any, back_ref, back_sem)
    into_copies = copy_parts(into_any, into_ref, load_sems.at[0])
    taps_copies = copy_parts(taps_any, taps_ref, load_sems.at[1])
    saved_copies = copy_parts(saved_any, saved_ref, load_sems.at[2])
    stages = [list(copies) for copies in zip(into_copies, taps_copies, saved_copies)]
    begin(field_copies + stages[0])
    slots, places = window_order(lengths_ref)
    spread(field_ref, wide_ref, field_copies)
    begin(stages[1] + stages[2])
    take_windows(wide_ref, part_ref, slots)
    for low in range(0, size, TILE):
        part, start = divmod(low * parts, size)
        if start == 0:
            finished(stages[part])
            begin({0: stages[3], 1: [back_copy]}.get(part, []))
        mid, high = low + TILE // 2, low + TILE
        tap_re = taps_ref[low:mid].astype(jnp.float32)
        tap_im = taps_ref[mid:high].astype(jnp.float32)
        cross_re, cross_im = 0.0, 0.0
        for slot, both in enumerate(transform_rows(into_ref, part_ref, low, width)):
            lanes = slice(slot * width, (slot + 1) * width)
            re, im = both[: TILE // 2], both[TILE // 2 :]
            spectra_ref[low:mid, lanes] = (tap_re * re + tap_im * im).astype(jnp.bfloat16)
            spectra_ref[mid:high, lanes] = (tap_re * im - tap_im * re).astype(jnp.bfloat16)
            old_re = saved_ref[low:mid, lanes].astype(jnp.float32)
            old_im = saved_ref[mid:high, lanes].astype(jnp.float32)
            cross_re += re * old_re + im * old_im
            cross_im += im * old_re - re * old_im
        spectra_ref[low:mid, 3 * width :] = cross_re.astype(jnp.bfloat16)
        spectra_ref[mid:high, 3 * width :] = cross_im.astype(jnp.bfloat16)
    back_copy.wait()
    for low in range(0, reach, STRIP):
        rows = slice(low, low + STRIP)
        if low < reach // 2:
            short = jnp.dot(
                back_ref[rows], spectra_ref[:, 2 * width :], preferred_element_type=jnp.float32
            )
            hold_rows(held_ref, 2, low, short[:, :width])
            terms = short[:, width:]
        else:
            terms = jnp.dot(
                back_ref[rows], spectra_ref[:, 3 * width :], preferred_element_type=jnp.float32
            )
        filter_ref[rows] = terms.astype(jnp.bfloat16)

    targets = (own_any, one_any, two_any, three_any)
    height = own_any.shape[0]
    chip = lax.axis_index("dp") // 2

    def each_block(act):
        for block in range(len(targets)):
            rows = pl.ds(block * height, height)
            for slot, target in enumerate(targets):

                @pl.when((chip ^ block) == slot)
                def _():
                    act(
                        pltpu.make_async_copy(filter_ref.at[rows], target, filter_sems.at[block])
                    )

    each_block(lambda copy: copy.start())
    for low in range(0, reach, STRIP):
        long = jnp.dot(
            back_ref[low : low + STRIP],
            spectra_ref[:, : 2 * width],
            preferred_element_type=jnp.float32,
        )
        hold_rows(held_ref, 0, low, long[:, :width])
        hold_rows(held_ref, 1, low, long[:, width:])
    place_windows(held_ref, wide_ref, places)
    finish(field_ref, gain_ref, wide_ref, out_ref, out_any, out_sems)
    each_block(lambda copy: copy.wait())


def backward_mix(delta, taps_spec, saved, gain, lengths, into, back, slices):
    rows, width = delta.shape
    size, reach = into.shape
    windows = lengths.shape[1]
    chips = slices // 2
    block = pltpu.HBM((reach // chips, width), jnp.bfloat16)
    return pl.pallas_call(
        backward_kernel,
        in_specs=[SCALARS, FAR, LOCAL] + [FAR] * 4,
        out_specs=[FAR] * (1 + chips),
        out_shape=[pltpu.HBM((rows, width), jnp.bfloat16)] + [block] * chips,
        scratch_shapes=[
            pltpu.VMEM((rows, width), jnp.bfloat16),
            pltpu.VMEM((size, reach), jnp.bfloat16),
            pltpu.VMEM((reach, size), jnp.bfloat16),
            pltpu.VMEM((size, width), jnp.bfloat16),
            pltpu.VMEM((rows, width), jnp.bfloat16),
            pltpu.VMEM((size, windows * width), jnp.bfloat16),
            pltpu.VMEM((reach, width), jnp.bfloat16),
            pltpu.VMEM((reach, windows * width), jnp.bfloat16),
            pltpu.VMEM((size, (windows + 1) * width), jnp.bfloat16),
            pltpu.VMEM((windows, width // LANES, reach, LANES), jnp.float32),
            pltpu.VMEM((width // LANES, rows + reach // 2, LANES), jnp.float32),
            pltpu.SemaphoreType.DMA((4,)),
            pltpu.SemaphoreType.DMA,
            pltpu.SemaphoreType.DMA((3, 4)),
            pltpu.SemaphoreType.DMA((chips,)),
            pltpu.SemaphoreType.DMA((4,)),
        ],
        compiler_params=params(40),
        cost_estimate=cost(7 * rows * size * width, 4 * rows * size + 16 * size * width),
        name="backward_mix",
    )(
        lengths, far(delta), gain, far(into), far(back), far(taps_spec), far(saved)
    )


def total_kernel(own_ref, *refs):
    total = own_ref[...]
    for come_ref in refs[:-1]:
        total = total + come_ref[...].astype(jnp.float32)
    refs[-1][...] = total * (1.0 / (2 * len(refs)))


def total_blocks(own, come):
    return pl.pallas_call(
        total_kernel,
        in_specs=[LOCAL] * (1 + len(come)),
        out_specs=LOCAL,
        out_shape=jax.ShapeDtypeStruct(own.shape, jnp.float32),
        compiler_params=params(4),
        name="total_blocks",
    )(own, *come)


def merge_kernel(own_ref, one_ref, two_ref, three_ref, kept_ref, away_ref, held_ref):
    terms = [ref[...].astype(jnp.float32) for ref in (own_ref, one_ref, two_ref, three_ref)]
    held_ref[...] = (terms[0] + terms[1]) + (terms[2] + terms[3])
    height = kept_ref.shape[0]
    core = lax.axis_index("dp") % 2
    kept_ref[...] = held_ref[pl.ds(pl.multiple_of(core * height, height), height)]
    away = held_ref[pl.ds(pl.multiple_of((1 - core) * height, height), height)]
    away_ref[...] = away.astype(jnp.bfloat16)


def merge_blocks(own, came):
    height, width = own.shape
    return pl.pallas_call(
        merge_kernel,
        in_specs=[LOCAL] * (1 + len(came)),
        out_specs=[LOCAL] * 2,
        out_shape=[
            jax.ShapeDtypeStruct((height // 2, width), jnp.float32),
            jax.ShapeDtypeStruct((height // 2, width), jnp.bfloat16),
        ],
        scratch_shapes=[pltpu.VMEM((height, width), jnp.float32)],
        compiler_params=params(4),
        name="merge_blocks",
    )(own, *came)


def total_kernel(kept_ref, come_ref, out_ref):
    out_ref[...] = (kept_ref[...] + come_ref[...].astype(jnp.float32)) * (1.0 / 8)


def total_blocks(kept, come):
    return pl.pallas_call(
        total_kernel,
        in_specs=[LOCAL] * 2,
        out_specs=LOCAL,
        out_shape=jax.ShapeDtypeStruct(kept.shape, jnp.float32),
        compiler_params=params(4),
        name="total_blocks",
    )(kept, come)


def swap(pieces):
    return lax.all_to_all(pieces, "ctx", split_axis=0, concat_axis=0, tiled=True)


def from_core(away):
    count = lax.axis_size("dp")
    return lax.ppermute(away, "dp", [(i, i ^ 1) for i in range(count)])


def from_chips(blocks):
    count = lax.axis_size("dp")
    return [
        lax.ppermute(block, "dp", [(i, i ^ (2 * step)) for i in range(count)])
        for step, block in enumerate(blocks, 1)
    ]


def shards(queries, key_inputs, value_inputs, cotangent, filter_taps, skip_gain, lengths):
    groups = lax.axis_size("ctx")
    slices = lax.axis_size("dp")
    rows = queries.shape[1]
    total = rows * groups
    reach, width = filter_taps.shape
    into, back = transform_tables(reach)
    into, back = jnp.asarray(into), jnp.asarray(back)
    gain = skip_gain[None, :]
    product, delta, taps_spec = opening(
        key_inputs[0], value_inputs[0], cotangent[0], queries[0], filter_taps, into, groups
    )
    product_cols = swap(product)
    delta, taps_spec = second(cotangent[0], queries[0], filter_taps, into, delta, taps_spec)
    delta_cols = swap(delta)
    mixing, saved = forward_mix(
        product_cols.reshape(total, width), taps_spec, gain, lengths, into, back
    )
    mixing_rows = swap(mixing.reshape(groups, rows, width))
    units, own, *blocks = backward_mix(
        delta_cols.reshape(total, width), taps_spec, saved, gain, lengths, into, back, slices
    )
    units_rows = swap(units.reshape(groups, rows, width))
    came = from_chips(blocks)
    mixed_out, query_grad, key_near = gate_both(
        mixing_rows, queries[0], cotangent[0], key_inputs[0]
    )
    *came, mixed_out = lax.optimization_barrier((*came, mixed_out))
    kept, away = merge_blocks(own, came)
    filter_grad = total_blocks(kept, from_core(away))
    units_rows, filter_grad = lax.optimization_barrier((units_rows, filter_grad))
    key_grad, value_grad = gate_last(units_rows, value_inputs[0], key_near)
    return (mixed_out[None], query_grad[None], key_grad[None], value_grad[None], filter_grad)


def solution(mesh):
    rows_spec = P("dp", "ctx", None)
    in_specs = (rows_spec,) * 4 + (P(None, "ctx"), P("ctx"), P("dp", None))
    out_specs = (rows_spec,) * 4 + (P("dp", "ctx"),)
    return jax.shard_map(shards, mesh=mesh, in_specs=in_specs, out_specs=out_specs, check_vma=False)
```

```python
import math

import jax
import jax.numpy as jnp
import numpy as np
from jax import lax
from jax.experimental import pallas as pl
from jax.experimental.pallas import tpu as pltpu
from jax.sharding import PartitionSpec as P

MIB = 1024 * 1024
LANES = 128
TILE = 256
STRIP = 512
FAR = pl.BlockSpec(memory_space=pltpu.HBM)
SCALARS = pl.BlockSpec(memory_space=pltpu.SMEM)
LOCAL = pl.BlockSpec(memory_space=pltpu.VMEM)


def transform_tables(reach):
    places = np.arange(reach)
    doubled = (2 * np.arange(reach)[:, None] + 1) * places[None, :] % (4 * reach)
    angle = doubled * (math.pi / (2 * reach))
    rows = np.stack([np.cos(angle), -np.sin(angle)], 0)
    rows = rows.reshape(2, 2 * reach // TILE, TILE // 2, reach).transpose(1, 0, 2, 3)
    rows = rows.reshape(2 * reach, reach)
    return rows.astype(jnp.bfloat16), (rows.T / reach).astype(jnp.bfloat16)


def cost(flops, nbytes):
    return pl.CostEstimate(flops=flops, bytes_accessed=nbytes, transcendentals=0)


def far(array):
    return pltpu.with_memory_space_constraint(array, pltpu.HBM)


def near(array):
    return pltpu.with_memory_space_constraint(array, pltpu.VMEM)


def params(mebibytes):
    return pltpu.CompilerParams(vmem_limit_bytes=mebibytes * MIB)


def pair_kernel(left_any, right_any, out_any, left_ref, right_ref, out_ref, sems):
    width = out_ref.shape[2]
    chunks = sems.shape[1]
    per = out_ref.shape[0] // chunks
    loads = []
    for chunk in range(chunks):
        cols = pl.ds(chunk * per * width, per * width)
        for index, (source, held) in enumerate(((left_any, left_ref), (right_any, right_ref))):
            copy = pltpu.make_async_copy(
                source.at[:, cols], held.at[:, cols], sems.at[index, chunk]
            )
            copy.start()
            loads.append(copy)
    stores = []
    for chunk in range(chunks):
        loads[2 * chunk].wait()
        loads[2 * chunk + 1].wait()
        for part in range(chunk * per, (chunk + 1) * per):
            cols = slice(part * width, (part + 1) * width)
            left = left_ref[:, cols].astype(jnp.float32)
            right = right_ref[:, cols].astype(jnp.float32)
            out_ref[part] = (left * right).astype(jnp.bfloat16)
        rows = pl.ds(chunk * per, per)
        copy = pltpu.make_async_copy(out_ref.at[rows], out_any.at[rows], sems.at[2, chunk])
        copy.start()
        stores.append(copy)
    for copy in stores:
        copy.wait()


def gate_kernel(
    inner_any, first_any, second_any, ahead_any, one_any, two_any, ahead_out,
    inner_ref, first_ref, second_ref, one_ref, two_ref, sems, hold_sem,
):
    groups, _, width = inner_ref.shape
    chunks = sems.shape[1]
    per = groups // chunks
    loads, stores = [], []
    for chunk in range(chunks):
        rows = pl.ds(chunk * per, per)
        cols = pl.ds(chunk * per * width, per * width)
        for copy in (
            pltpu.make_async_copy(inner_any.at[rows], inner_ref.at[rows], sems.at[0, chunk]),
            pltpu.make_async_copy(first_any.at[:, cols], first_ref.at[:, cols], sems.at[1, chunk]),
            pltpu.make_async_copy(second_any.at[:, cols], second_ref.at[:, cols], sems.at[2, chunk]),
        ):
            copy.start()
            loads.append(copy)
    copy = pltpu.make_async_copy(ahead_any, ahead_out, hold_sem)
    copy.start()
    stores.append(copy)
    for chunk in range(chunks):
        for copy in loads[3 * chunk : 3 * chunk + 3]:
            copy.wait()
        for part in range(chunk * per, (chunk + 1) * per):
            cols = slice(part * width, (part + 1) * width)
            inner = inner_ref[part].astype(jnp.float32)
            one_ref[:, cols] = (inner * first_ref[:, cols].astype(jnp.float32)).astype(jnp.bfloat16)
            two_ref[:, cols] = (inner * second_ref[:, cols].astype(jnp.float32)).astype(
                jnp.bfloat16
            )
        cols = pl.ds(chunk * per * width, per * width)
        for index, (held, target) in enumerate(((one_ref, one_any), (two_ref, two_any))):
            copy = pltpu.make_async_copy(
                held.at[:, cols], target.at[:, cols], sems.at[3 + index, chunk]
            )
            copy.start()
            stores.append(copy)
    for copy in stores:
        copy.wait()


def gate_both(inner, first, second, ahead):
    groups, rows, width = inner.shape
    columns = groups * width
    held = pltpu.VMEM((rows, columns), jnp.bfloat16)
    return pl.pallas_call(
        gate_kernel,
        in_specs=[pl.BlockSpec(memory_space=pl.ANY)] + [FAR] * 3,
        out_specs=[FAR] * 2 + [LOCAL],
        out_shape=[pltpu.HBM((rows, columns), jnp.bfloat16)] * 2 + [held],
        scratch_shapes=[
            pltpu.VMEM((groups, rows, width), jnp.bfloat16),
            held, held, held, held,
            pltpu.SemaphoreType.DMA((5, 4)),
            pltpu.SemaphoreType.DMA,
        ],
        compiler_params=params(12),
        cost_estimate=cost(2 * rows * columns, 12 * rows * columns),
        name="gate_both",
    )(inner, far(first), far(second), far(ahead))


def last_kernel(
    inner_ref, first_any, second_ref, one_any, two_any, first_ref, one_ref, two_ref, sems
):
    groups, _, width = inner_ref.shape
    chunks = sems.shape[1]
    per = groups // chunks
    loads, stores = [], []
    for chunk in range(chunks):
        cols = pl.ds(chunk * per * width, per * width)
        copy = pltpu.make_async_copy(first_any.at[:, cols], first_ref.at[:, cols], sems.at[2, chunk])
        copy.start()
        loads.append(copy)
    for chunk in range(chunks):
        loads[chunk].wait()
        for part in range(chunk * per, (chunk + 1) * per):
            cols = slice(part * width, (part + 1) * width)
            inner = inner_ref[part].astype(jnp.float32)
            one_ref[:, cols] = (inner * first_ref[:, cols].astype(jnp.float32)).astype(jnp.bfloat16)
            two_ref[:, cols] = (inner * second_ref[:, cols].astype(jnp.float32)).astype(
                jnp.bfloat16
            )
        cols = pl.ds(chunk * per * width, per * width)
        for index, (held, target) in enumerate(((one_ref, one_any), (two_ref, two_any))):
            copy = pltpu.make_async_copy(held.at[:, cols], target.at[:, cols], sems.at[index, chunk])
            copy.start()
            stores.append(copy)
    for copy in stores:
        copy.wait()


def gate_last(inner, first, second):
    groups, rows, width = inner.shape
    columns = groups * width
    held = pltpu.VMEM((rows, columns), jnp.bfloat16)
    return pl.pallas_call(
        last_kernel,
        in_specs=[LOCAL, FAR, LOCAL],
        out_specs=[FAR] * 2,
        out_shape=[pltpu.HBM((rows, columns), jnp.bfloat16)] * 2,
        scratch_shapes=[held, held, held, pltpu.SemaphoreType.DMA((3, 4))],
        compiler_params=params(8),
        cost_estimate=cost(2 * rows * columns, 10 * rows * columns),
        name="gate_last",
    )(near(inner), far(first), near(second))


def taps_kernel(meanwhile, taps_any, into_any, out_any, taps_ref, into_ref, out_ref, sems):
    size = out_ref.shape[0]
    tiles = size // TILE
    first = pltpu.make_async_copy(taps_any, taps_ref, sems.at[0, 0])
    first.start()
    loads, stores = [], []
    for tile in range(tiles):
        rows = pl.ds(tile * TILE, TILE)
        copy = pltpu.make_async_copy(into_any.at[rows], into_ref.at[rows], sems.at[1, tile])
        copy.start()
        loads.append(copy)
    meanwhile()
    first.wait()
    taps = taps_ref[...].astype(jnp.bfloat16)
    for tile in range(tiles):
        rows = slice(tile * TILE, (tile + 1) * TILE)
        loads[tile].wait()
        part = jnp.dot(into_ref[rows], taps, preferred_element_type=jnp.float32)
        out_ref[rows] = part.astype(jnp.bfloat16)
        rows = pl.ds(tile * TILE, TILE)
        copy = pltpu.make_async_copy(out_ref.at[rows], out_any.at[rows], sems.at[2, tile])
        copy.start()
        stores.append(copy)
    for copy in stores:
        copy.wait()


def opening_kernel(
    key_any, value_any, cot_any, query_any, taps_any, into_any,
    product_any, delta_any, spectrum_any,
    left_ref, right_ref, pair_ref, pair_sems, taps_ref, into_ref, spectrum_ref, taps_sems,
):
    pair = (left_ref, right_ref, pair_ref, pair_sems)
    pair_kernel(key_any, value_any, product_any, *pair)

    @pl.when(lax.axis_index("dp") % 2 == 1)
    def _():
        taps_kernel(
            lambda: pair_kernel(cot_any, query_any, delta_any, *pair),
            taps_any, into_any, spectrum_any, taps_ref, into_ref, spectrum_ref, taps_sems,
        )


def second_kernel(
    cot_any, query_any, taps_any, into_any, _, __, delta_any, spectrum_any,
    left_ref, right_ref, pair_ref, pair_sems, taps_ref, into_ref, spectrum_ref, taps_sems,
):
    @pl.when(lax.axis_index("dp") % 2 == 0)
    def _():
        pair = (left_ref, right_ref, pair_ref, pair_sems)
        taps_kernel(
            lambda: pair_kernel(cot_any, query_any, delta_any, *pair),
            taps_any, into_any, spectrum_any, taps_ref, into_ref, spectrum_ref, taps_sems,
        )


def opening_scratch(rows, columns, groups, reach, size, width):
    return [
        pltpu.VMEM((rows, columns), jnp.bfloat16),
        pltpu.VMEM((rows, columns), jnp.bfloat16),
        pltpu.VMEM((groups, rows, columns // groups), jnp.bfloat16),
        pltpu.SemaphoreType.DMA((3, 4)),
        pltpu.VMEM((reach, width), jnp.float32),
        pltpu.VMEM((size, reach), jnp.bfloat16),
        pltpu.VMEM((size, width), jnp.bfloat16),
        pltpu.SemaphoreType.DMA((3, size // TILE)),
    ]


def opening(key, value, cotangent, queries, taps, into, groups):
    rows, columns = key.shape
    reach, width = taps.shape
    size = into.shape[0]
    pieces = pltpu.HBM((groups, rows, columns // groups), jnp.bfloat16)
    return pl.pallas_call(
        opening_kernel,
        in_specs=[FAR] * 6,
        out_specs=[FAR] * 3,
        out_shape=[pieces, pieces, pltpu.HBM((size, width), jnp.bfloat16)],
        scratch_shapes=opening_scratch(rows, columns, groups, reach, size, width),
        compiler_params=params(20),
        cost_estimate=cost(rows * columns, 6 * rows * columns),
        name="opening",
    )(far(key), far(value), far(cotangent), far(queries), far(taps), far(into))


def second(cotangent, queries, taps, into, delta, spectrum):
    rows, columns = queries.shape
    reach, width = taps.shape
    size = into.shape[0]
    groups = delta.shape[0]
    return pl.pallas_call(
        second_kernel,
        in_specs=[FAR] * 6,
        out_specs=[FAR] * 2,
        out_shape=[pltpu.HBM(delta.shape, delta.dtype), pltpu.HBM(spectrum.shape, spectrum.dtype)],
        input_output_aliases={4: 0, 5: 1},
        scratch_shapes=opening_scratch(rows, columns, groups, reach, size, width),
        compiler_params=params(20),
        cost_estimate=cost(2 * reach * size * width, 2 * reach * size + 4 * size * width),
        name="second",
    )(far(cotangent), far(queries), far(taps), far(into), far(delta), far(spectrum))


def window_order(lengths_ref):
    lengths = [lengths_ref[0, window] for window in range(3)]
    starts = [jnp.int32(0), lengths[0], lengths[0] + lengths[1]]
    first = (lengths[0] >= lengths[1]) & (lengths[0] >= lengths[2])
    second = ~first & (lengths[1] >= lengths[2])
    longest = jnp.where(first, 0, jnp.where(second, 1, 2))
    low = jnp.where(longest == 0, 1, 0)
    high = jnp.where(longest == 2, 1, 2)
    pick = lambda values, index: jnp.where(
        index == 0, values[0], jnp.where(index == 1, values[1], values[2])
    )
    swapped = pick(lengths, low) < pick(lengths, high)
    middle = jnp.where(swapped, high, low)
    shortest = jnp.where(swapped, low, high)
    slots = [(pick(starts, index), pick(lengths, index)) for index in (longest, middle, shortest)]
    places = [
        (
            jnp.where(longest == window, 0, jnp.where(middle == window, 1, 2)),
            starts[window],
            lengths[window],
        )
        for window in range(3)
    ]
    return slots, places


def spread(field_ref, wide_ref, copies):
    step = field_ref.shape[0] // len(copies)
    for part, copy in enumerate(copies):
        rows = slice(part * step, (part + 1) * step)
        copy.wait()
        for half in range(wide_ref.shape[0]):
            lanes = slice(half * LANES, (half + 1) * LANES)
            wide_ref[half, rows] = field_ref[rows, lanes].astype(jnp.float32)


def take_windows(wide_ref, part_ref, slots):
    reach = part_ref.shape[0]
    for slot, (start, length) in enumerate(slots):
        rows = reach // 2 if slot == 2 else reach
        inside = lax.broadcasted_iota(jnp.int32, (rows, LANES), 0) < length
        for half in range(wide_ref.shape[0]):
            lane = (slot * wide_ref.shape[0] + half) * LANES
            part = wide_ref[half, pl.ds(start, rows)]
            if slot > 0:
                part = jnp.where(inside, part, 0.0)
            part_ref[:rows, lane : lane + LANES] = part.astype(jnp.bfloat16)


def transform_rows(into_ref, part_ref, low, width):
    reach = part_ref.shape[0]
    rows = slice(low, low + TILE)
    long = jnp.dot(into_ref[rows], part_ref[:, : 2 * width], preferred_element_type=jnp.float32)
    short = jnp.dot(
        into_ref[rows, : reach // 2],
        part_ref[: reach // 2, 2 * width :],
        preferred_element_type=jnp.float32,
    )
    return long[:, :width], long[:, width:], short


def place_windows(held_ref, wide_ref, places):
    reach = held_ref.shape[2]
    for slot, start, length in places:

        def body(rows):
            for half in range(wide_ref.shape[0]):
                wide_ref[half, pl.ds(start, rows)] = held_ref[slot, half, :rows]

        @pl.when(length > reach // 2)
        def _():
            body(reach)

        @pl.when(length <= reach // 2)
        def _():
            body(reach // 2)


def hold_rows(held_ref, slot, low, part):
    for half in range(held_ref.shape[1]):
        lanes = slice(half * LANES, (half + 1) * LANES)
        held_ref[slot, half, low : low + part.shape[0]] = part[:, lanes]


def finish(field_ref, gain_ref, wide_ref, out_ref, out_any, sem):
    rows = out_ref.shape[0]
    step = rows // sem.shape[0]
    copies = []
    for index in range(sem.shape[0]):
        place = slice(index * step, (index + 1) * step)
        for half in range(wide_ref.shape[0]):
            lanes = slice(half * LANES, (half + 1) * LANES)
            direct = gain_ref[:, lanes] * field_ref[place, lanes].astype(jnp.float32)
            out_ref[place, lanes] = (wide_ref[half, place] + direct).astype(jnp.bfloat16)
        place = pl.ds(index * step, step)
        copy = pltpu.make_async_copy(out_ref.at[place], out_any.at[place], sem.at[index])
        copy.start()
        copies.append(copy)
    for copy in copies:
        copy.wait()


def copy_parts(source, held, sems):
    parts = sems.shape[0]
    step = source.shape[0] // parts
    copies = []
    for part in range(parts):
        rows = pl.ds(part * step, step)
        copies.append(pltpu.make_async_copy(source.at[rows], held.at[rows], sems.at[part]))
    return copies


def begin(copies):
    for copy in copies:
        copy.start()


def finished(copies):
    for copy in copies:
        copy.wait()


def forward_kernel(
    lengths_ref, field_any, gain_ref, into_any, back_any, taps_any, out_any, saved_any,
    field_ref, into_ref, back_ref, taps_ref, out_ref, saved_ref,
    part_ref, spectra_ref, held_ref, wide_ref, field_sems, back_sem, load_sems, out_sems,
):
    size, reach = into_ref.shape
    width = taps_ref.shape[1]
    parts = load_sems.shape[1]
    field_copies = copy_parts(field_any, field_ref, field_sems)
    back_copy = pltpu.make_async_copy(back_any, back_ref, back_sem)
    into_copies = copy_parts(into_any, into_ref, load_sems.at[0])
    taps_copies = copy_parts(taps_any, taps_ref, load_sems.at[1])
    saved_copies = copy_parts(saved_ref, saved_any, load_sems.at[2])
    stages = [list(copies) for copies in zip(into_copies, taps_copies)]
    begin(field_copies + stages[0])
    slots, places = window_order(lengths_ref)
    spread(field_ref, wide_ref, field_copies)
    begin(stages[1] + stages[2])
    take_windows(wide_ref, part_ref, slots)
    for low in range(0, size, TILE):
        part, start = divmod(low * parts, size)
        if start == 0:
            finished(stages[part])
            begin({0: stages[3], 1: [back_copy]}.get(part, []))
        mid, high = low + TILE // 2, low + TILE
        tap_re = taps_ref[low:mid].astype(jnp.float32)
        tap_im = taps_ref[mid:high].astype(jnp.float32)
        for slot, both in enumerate(transform_rows(into_ref, part_ref, low, width)):
            lanes = slice(slot * width, (slot + 1) * width)
            re, im = both[: TILE // 2], both[TILE // 2 :]
            saved_ref[low:high, lanes] = both.astype(jnp.bfloat16)
            spectra_ref[low:mid, lanes] = (tap_re * re - tap_im * im).astype(jnp.bfloat16)
            spectra_ref[mid:high, lanes] = (tap_re * im + tap_im * re).astype(jnp.bfloat16)
        if start + TILE * parts == size:
            begin([saved_copies[part]])
    back_copy.wait()
    for low in range(0, reach, STRIP):
        long = jnp.dot(
            back_ref[low : low + STRIP],
            spectra_ref[:, : 2 * width],
            preferred_element_type=jnp.float32,
        )
        hold_rows(held_ref, 0, low, long[:, :width])
        hold_rows(held_ref, 1, low, long[:, width:])
    short = jnp.dot(
        back_ref[: reach // 2], spectra_ref[:, 2 * width :], preferred_element_type=jnp.float32
    )
    hold_rows(held_ref, 2, 0, short)
    place_windows(held_ref, wide_ref, places)
    finish(field_ref, gain_ref, wide_ref, out_ref, out_any, out_sems)
    finished(saved_copies)


def forward_mix(product, taps_spec, gain, lengths, into, back):
    rows, width = product.shape
    size, reach = into.shape
    windows = lengths.shape[1]
    return pl.pallas_call(
        forward_kernel,
        in_specs=[SCALARS, FAR, LOCAL, FAR, FAR, FAR],
        out_specs=[FAR] * 2,
        out_shape=[
            pltpu.HBM((rows, width), jnp.bfloat16),
            pltpu.HBM((size, windows * width), jnp.bfloat16),
        ],
        scratch_shapes=[
            pltpu.VMEM((rows, width), jnp.bfloat16),
            pltpu.VMEM((size, reach), jnp.bfloat16),
            pltpu.VMEM((reach, size), jnp.bfloat16),
            pltpu.VMEM((size, width), jnp.bfloat16),
            pltpu.VMEM((rows, width), jnp.bfloat16),
            pltpu.VMEM((size, windows * width), jnp.bfloat16),
            pltpu.VMEM((reach, windows * width), jnp.bfloat16),
            pltpu.VMEM((size, windows * width), jnp.bfloat16),
            pltpu.VMEM((windows, width // LANES, reach, LANES), jnp.float32),
            pltpu.VMEM((width // LANES, rows + reach // 2, LANES), jnp.float32),
            pltpu.SemaphoreType.DMA((4,)),
            pltpu.SemaphoreType.DMA,
            pltpu.SemaphoreType.DMA((3, 4)),
            pltpu.SemaphoreType.DMA((4,)),
        ],
        compiler_params=params(40),
        cost_estimate=cost(6 * rows * size * width, 4 * rows * size + 16 * size * width),
        name="forward_mix",
    )(lengths, far(product), gain, far(into), far(back), far(taps_spec))


def backward_kernel(
    lengths_ref, field_any, gain_ref, into_any, back_any, taps_any, saved_any,
    out_any, own_any, one_any, two_any, three_any,
    field_ref, into_ref, back_ref, taps_ref, out_ref, saved_ref, filter_ref,
    part_ref, spectra_ref, held_ref, wide_ref, field_sems, back_sem, load_sems, filter_sems, out_sems,
):
    size, reach = into_ref.shape
    width = taps_ref.shape[1]
    parts = load_sems.shape[1]
    field_copies = copy_parts(field_any, field_ref, field_sems)
    back_copy = pltpu.make_async_copy(back_any, back_ref, back_sem)
    into_copies = copy_parts(into_any, into_ref, load_sems.at[0])
    taps_copies = copy_parts(taps_any, taps_ref, load_sems.at[1])
    saved_copies = copy_parts(saved_any, saved_ref, load_sems.at[2])
    stages = [list(copies) for copies in zip(into_copies, taps_copies, saved_copies)]
    begin(field_copies + stages[0])
    slots, places = window_order(lengths_ref)
    spread(field_ref, wide_ref, field_copies)
    begin(stages[1] + stages[2])
    take_windows(wide_ref, part_ref, slots)
    for low in range(0, size, TILE):
        part, start = divmod(low * parts, size)
        if start == 0:
            finished(stages[part])
            begin({0: stages[3], 1: [back_copy]}.get(part, []))
        mid, high = low + TILE // 2, low + TILE
        tap_re = taps_ref[low:mid].astype(jnp.float32)
        tap_im = taps_ref[mid:high].astype(jnp.float32)
        cross_re, cross_im = 0.0, 0.0
        for slot, both in enumerate(transform_rows(into_ref, part_ref, low, width)):
            lanes = slice(slot * width, (slot + 1) * width)
            re, im = both[: TILE // 2], both[TILE // 2 :]
            spectra_ref[low:mid, lanes] = (tap_re * re + tap_im * im).astype(jnp.bfloat16)
            spectra_ref[mid:high, lanes] = (tap_re * im - tap_im * re).astype(jnp.bfloat16)
            old_re = saved_ref[low:mid, lanes].astype(jnp.float32)
            old_im = saved_ref[mid:high, lanes].astype(jnp.float32)
            cross_re += re * old_re + im * old_im
            cross_im += im * old_re - re * old_im
        spectra_ref[low:mid, 3 * width :] = cross_re.astype(jnp.bfloat16)
        spectra_ref[mid:high, 3 * width :] = cross_im.astype(jnp.bfloat16)
    back_copy.wait()
    for low in range(0, reach, STRIP):
        rows = slice(low, low + STRIP)
        if low < reach // 2:
            short = jnp.dot(
                back_ref[rows], spectra_ref[:, 2 * width :], preferred_element_type=jnp.float32
            )
            hold_rows(held_ref, 2, low, short[:, :width])
            terms = short[:, width:]
        else:
            terms = jnp.dot(
                back_ref[rows], spectra_ref[:, 3 * width :], preferred_element_type=jnp.float32
            )
        filter_ref[rows] = terms.astype(jnp.bfloat16)

    targets = (own_any, one_any, two_any, three_any)
    height = own_any.shape[0]
    chip = lax.axis_index("dp") // 2

    def each_block(act):
        for block in range(len(targets)):
            rows = pl.ds(block * height, height)
            for slot, target in enumerate(targets):

                @pl.when((chip ^ block) == slot)
                def _():
                    act(
                        pltpu.make_async_copy(filter_ref.at[rows], target, filter_sems.at[block])
                    )

    each_block(lambda copy: copy.start())
    for low in range(0, reach, STRIP):
        long = jnp.dot(
            back_ref[low : low + STRIP],
            spectra_ref[:, : 2 * width],
            preferred_element_type=jnp.float32,
        )
        hold_rows(held_ref, 0, low, long[:, :width])
        hold_rows(held_ref, 1, low, long[:, width:])
    place_windows(held_ref, wide_ref, places)
    finish(field_ref, gain_ref, wide_ref, out_ref, out_any, out_sems)
    each_block(lambda copy: copy.wait())


def backward_mix(delta, taps_spec, saved, gain, lengths, into, back, slices):
    rows, width = delta.shape
    size, reach = into.shape
    windows = lengths.shape[1]
    chips = slices // 2
    block = pltpu.HBM((reach // chips, width), jnp.bfloat16)
    return pl.pallas_call(
        backward_kernel,
        in_specs=[SCALARS, FAR, LOCAL] + [FAR] * 4,
        out_specs=[FAR] * (1 + chips),
        out_shape=[pltpu.HBM((rows, width), jnp.bfloat16)] + [block] * chips,
        scratch_shapes=[
            pltpu.VMEM((rows, width), jnp.bfloat16),
            pltpu.VMEM((size, reach), jnp.bfloat16),
            pltpu.VMEM((reach, size), jnp.bfloat16),
            pltpu.VMEM((size, width), jnp.bfloat16),
            pltpu.VMEM((rows, width), jnp.bfloat16),
            pltpu.VMEM((size, windows * width), jnp.bfloat16),
            pltpu.VMEM((reach, width), jnp.bfloat16),
            pltpu.VMEM((reach, windows * width), jnp.bfloat16),
            pltpu.VMEM((size, (windows + 1) * width), jnp.bfloat16),
            pltpu.VMEM((windows, width // LANES, reach, LANES), jnp.float32),
            pltpu.VMEM((width // LANES, rows + reach // 2, LANES), jnp.float32),
            pltpu.SemaphoreType.DMA((4,)),
            pltpu.SemaphoreType.DMA,
            pltpu.SemaphoreType.DMA((3, 4)),
            pltpu.SemaphoreType.DMA((chips,)),
            pltpu.SemaphoreType.DMA((4,)),
        ],
        compiler_params=params(40),
        cost_estimate=cost(7 * rows * size * width, 4 * rows * size + 16 * size * width),
        name="backward_mix",
    )(
        lengths, far(delta), gain, far(into), far(back), far(taps_spec), far(saved)
    )


def total_kernel(own_ref, *refs):
    total = own_ref[...]
    for come_ref in refs[:-1]:
        total = total + come_ref[...].astype(jnp.float32)
    refs[-1][...] = total * (1.0 / (2 * len(refs)))


def total_blocks(own, come):
    return pl.pallas_call(
        total_kernel,
        in_specs=[LOCAL] * (1 + len(come)),
        out_specs=LOCAL,
        out_shape=jax.ShapeDtypeStruct(own.shape, jnp.float32),
        compiler_params=params(4),
        name="total_blocks",
    )(own, *come)


def merge_kernel(own_ref, one_ref, two_ref, three_ref, kept_ref, away_ref, held_ref):
    terms = [ref[...].astype(jnp.float32) for ref in (own_ref, one_ref, two_ref, three_ref)]
    held_ref[...] = (terms[0] + terms[1]) + (terms[2] + terms[3])
    height = kept_ref.shape[0]
    core = lax.axis_index("dp") % 2
    kept_ref[...] = held_ref[pl.ds(pl.multiple_of(core * height, height), height)]
    away = held_ref[pl.ds(pl.multiple_of((1 - core) * height, height), height)]
    away_ref[...] = away.astype(jnp.bfloat16)


def merge_blocks(own, came):
    height, width = own.shape
    return pl.pallas_call(
        merge_kernel,
        in_specs=[LOCAL] * (1 + len(came)),
        out_specs=[LOCAL] * 2,
        out_shape=[
            jax.ShapeDtypeStruct((height // 2, width), jnp.float32),
            jax.ShapeDtypeStruct((height // 2, width), jnp.bfloat16),
        ],
        scratch_shapes=[pltpu.VMEM((height, width), jnp.float32)],
        compiler_params=params(4),
        name="merge_blocks",
    )(own, *came)


def total_kernel(kept_ref, come_ref, out_ref):
    out_ref[...] = (kept_ref[...] + come_ref[...].astype(jnp.float32)) * (1.0 / 8)


def total_blocks(kept, come):
    return pl.pallas_call(
        total_kernel,
        in_specs=[LOCAL] * 2,
        out_specs=LOCAL,
        out_shape=jax.ShapeDtypeStruct(kept.shape, jnp.float32),
        compiler_params=params(4),
        name="total_blocks",
    )(kept, come)


def swap(pieces):
    return lax.all_to_all(pieces, "ctx", split_axis=0, concat_axis=0, tiled=True)


def from_core(away):
    count = lax.axis_size("dp")
    return lax.ppermute(away, "dp", [(i, i ^ 1) for i in range(count)])


def from_chips(blocks):
    count = lax.axis_size("dp")
    return [
        lax.ppermute(block, "dp", [(i, i ^ (2 * step)) for i in range(count)])
        for step, block in enumerate(blocks, 1)
    ]


def shards(queries, key_inputs, value_inputs, cotangent, filter_taps, skip_gain, lengths):
    groups = lax.axis_size("ctx")
    slices = lax.axis_size("dp")
    rows = queries.shape[1]
    total = rows * groups
    reach, width = filter_taps.shape
    into, back = transform_tables(reach)
    into, back = jnp.asarray(into), jnp.asarray(back)
    gain = skip_gain[None, :]
    product, delta, taps_spec = opening(
        key_inputs[0], value_inputs[0], cotangent[0], queries[0], filter_taps, into, groups
    )
    product_cols = swap(product)
    delta, taps_spec = second(cotangent[0], queries[0], filter_taps, into, delta, taps_spec)
    delta_cols = swap(delta)
    mixing, saved = forward_mix(
        product_cols.reshape(total, width), taps_spec, gain, lengths, into, back
    )
    mixing_rows = swap(mixing.reshape(groups, rows, width))
    units, own, *blocks = backward_mix(
        delta_cols.reshape(total, width), taps_spec, saved, gain, lengths, into, back, slices
    )
    units_rows = swap(units.reshape(groups, rows, width))
    came = from_chips(blocks)
    mixed_out, query_grad, key_near = gate_both(
        mixing_rows, queries[0], cotangent[0], key_inputs[0]
    )
    *came, mixed_out = lax.optimization_barrier((*came, mixed_out))
    kept, away = merge_blocks(own, came)
    filter_grad = total_blocks(kept, from_core(away))
    units_rows, filter_grad = lax.optimization_barrier((units_rows, filter_grad))
    key_grad, value_grad = gate_last(units_rows, value_inputs[0], key_near)
    return (mixed_out[None], query_grad[None], key_grad[None], value_grad[None], filter_grad)


def solution(mesh):
    rows_spec = P("dp", "ctx", None)
    in_specs = (rows_spec,) * 4 + (P(None, "ctx"), P("ctx"), P("dp", None))
    out_specs = (rows_spec,) * 4 + (P("dp", "ctx"),)
    return jax.shard_map(shards, mesh=mesh, in_specs=in_specs, out_specs=out_specs, check_vma=False)
```
